256 devices in a mesh: row: 32 (over y, z), col: 8 (over x, core).
Axes of the slice: x: 4, y: 4, z: 8, core: 2. Of those that a mesh axis runs over, the one named last changes fastest.
Arguments:
- param_up: float32 [4096, 16384], P('row', 'col'), may hold values from -0.09375 to 0.09375
- grad_up: bfloat16 [4096, 16384], P('row', 'col'), as said below
- mom_up: bfloat16 [4096, 16384], P('row', 'col'), may hold values from -6 to 6
- rows_up: float32 [4096], P('row'), may hold values from 500 to 45000, as said below
- cols_up: float32 [16384], P('col'), may hold values from 0.5 to 5000
- param_attn: float32 [4096, 4096], P('row', 'col'), may hold values from -0.09375 to 0.09375
- grad_attn: bfloat16 [4096, 4096], P('row', 'col'), as said below
- mom_attn: bfloat16 [4096, 4096], P('row', 'col'), may hold values from -6 to 6
- rows_attn: float32 [4096], P('row'), may hold values from 500 to 45000, as said below
- cols_attn: float32 [4096], P('col'), may hold values from 0.5 to 5000
Outputs:
- new_param_up: float32 [4096, 16384], P('row', 'col')
- new_mom_up: bfloat16 [4096, 16384], P('row', 'col')
- new_rows_up: float32 [4096], P('row')
- new_cols_up: float32 [16384], P('col')
- copy_up: bfloat16 [4096, 16384], P('row')
- new_param_attn: float32 [4096, 4096], P('row', 'col')
- new_mom_attn: bfloat16 [4096, 4096], P('row', 'col')
- new_rows_attn: float32 [4096], P('row')
- new_cols_attn: float32 [4096], P('col')
- copy_attn: bfloat16 [4096, 4096], P('row')
- mean_logs: float32 [4], replicated
The draws below stay inside these ranges and needn't reach their ends.
Inputs may be any that keep to these rules, and one draw needn't show every extreme that they name: `grad_up`: finite gradient entries. `grad_attn`: finite gradient entries. `rows_up`: positive entries. `rows_attn`: positive entries.
All inputs are finite; a program needn't handle non-finite values.
Results may differ from the reference program's by a relative error of at most 0.0075.
Values may be sent and summed in bfloat16 or wider, within the bound.
A program may use at most 64 MiB of HBM per device.

```python
import math
import jax
import jax.numpy as jnp
from jax import lax

D = 4096
FF = 16384


def scaled_grad(key, rows, cols, base, top):
    key_row, key_col, key_band, key_own = jax.random.split(key, 4)
    bands = min(32, rows)
    row_scale = jnp.exp(jax.random.uniform(key_row, (rows, 1), jnp.float32) * jnp.log(top))
    strength = jax.random.uniform(key_band, (bands, 1), jnp.float32)
    shared = jax.random.uniform(key_col, (1, cols), jnp.float32)
    own = jax.random.uniform(key_own, (bands, cols), jnp.float32)
    table = jnp.exp((strength * shared + 0.6 * own) * jnp.log(top))
    col_scale = jnp.repeat(table, rows // bands, axis=0)
    row_ramp = 1.0 + 2.0 * jnp.arange(rows, dtype=jnp.float32)[:, None] / max(rows - 1, 1)
    col_ramp = 1.0 + 2.0 * jnp.arange(cols, dtype=jnp.float32)[None, :] / max(cols - 1, 1)
    return base * row_scale * col_scale * row_ramp * col_ramp


def rising_stat(key, count, power):
    spread = jnp.exp(jax.random.uniform(key, (count,), jnp.float32) * jnp.log(10.0)) * 500.0
    ramp = 1.0 + 2.0 * jnp.arange(count, dtype=jnp.float32) / max(count - 1, 1)
    return spread * ramp ** power


def draw_rows_up(key, part):
    key = jax.random.fold_in(key, 37)
    return rising_stat(key, D, 1.0)


def draw_rows_attn(key, part):
    key = jax.random.fold_in(key, 41)
    return rising_stat(key, D, 1.0)


def draw_grad_up(key, part):
    key = jax.random.fold_in(key, 11)
    key_base, key_scale = jax.random.split(key, 2)
    base = jax.random.normal(key_base, (D, FF), jnp.float32)
    top = 10.0
    return scaled_grad(key_scale, D, FF, base, top).astype(jnp.bfloat16)


def draw_grad_attn(key, part):
    key = jax.random.fold_in(key, 23)
    key_base, key_scale = jax.random.split(key, 2)
    base = jax.random.normal(key_base, (D, D), jnp.float32)
    top = 10.0
    return scaled_grad(key_scale, D, D, base, top).astype(jnp.bfloat16)


def shard_levels(key, shape, cuts, low, top_value):
    level, own = 1.0, jax.random.fold_in(key, 6)
    for axis_at, parts in cuts:
        heights = jnp.exp(jax.random.uniform(jax.random.fold_in(own, axis_at), (parts,), jnp.float32, low / len(cuts), top_value / len(cuts)))
        level = level * jnp.repeat(heights, shape[axis_at] // parts).reshape([-1 if axis == axis_at else 1 for axis in range(len(shape))])
    return level


def bell_draw(rng, shape, scale, limit, cuts=(), kind=jnp.bfloat16):
    values = scale * jax.random.normal(rng, shape, jnp.float32)
    if cuts:
        values = values * shard_levels(rng, shape, cuts, -0.22, 0.18)
    return jnp.clip(values, -limit, limit).astype(kind)


def setup_inputs(seed: int = 0) -> dict:
    key_of = jax.random.split(jax.random.key(seed), 11)
    return {
        "param_up": bell_draw(key_of[0], (D, FF), D ** -0.5, 0.09375, ((0, 32), (1, 8)), jnp.float32),
        "grad_up": draw_grad_up(jax.random.fold_in(key_of[10], 71), 0),
        "mom_up": bell_draw(key_of[2], (D, FF), 1.0, 6.0, ((0, 32), (1, 8))),
        "rows_up": draw_rows_up(jax.random.fold_in(key_of[10], 71), 0),
        "cols_up": jnp.clip(jnp.exp(math.log(5000.0) - 9.2103404 * jax.random.uniform(key_of[4], (FF,), jnp.float32) ** shard_levels(key_of[4], (FF,), ((0, 8),), -0.2, 0.2)), 0.5, 5000.0),
        "param_attn": bell_draw(key_of[5], (D, D), D ** -0.5, 0.09375, ((0, 32), (1, 8)), jnp.float32),
        "grad_attn": draw_grad_attn(jax.random.fold_in(key_of[10], 71), 0),
        "mom_attn": bell_draw(key_of[7], (D, D), 1.0, 6.0, ((0, 32), (1, 8))),
        "rows_attn": draw_rows_attn(jax.random.fold_in(key_of[10], 71), 0),
        "cols_attn": jnp.clip(jnp.exp(math.log(5000.0) - 9.2103404 * jax.random.uniform(key_of[9], (D,), jnp.float32) ** shard_levels(key_of[9], (D,), ((0, 8),), -0.2, 0.2)), 0.5, 5000.0),
    }


DECAY = 0.8415
BETA = 0.9
RATE = 0.01
TINY = 1e-30

def adafactor(param, grad, mom, rows, cols):
    wide = grad.astype(jnp.float32)
    squares = wide * wide + TINY
    n_rows = squares.shape[0]
    n_cols = squares.shape[1]
    new_rows = DECAY * rows + (1.0 - DECAY) * lax.optimization_barrier(jnp.sum(squares, axis=1)) / n_cols
    new_cols = DECAY * cols + (1.0 - DECAY) * lax.optimization_barrier(jnp.sum(squares, axis=0)) / n_rows
    row_mean = jnp.sum(new_rows) / n_rows
    update = wide / jnp.sqrt(new_rows[:, None] * new_cols[None, :] / row_mean)
    mean_square = jnp.sum(update * update) / (n_rows * n_cols)
    clip = 1.0 / jnp.maximum(1.0, jnp.sqrt(mean_square))
    new_mom = (BETA * mom.astype(jnp.float32) + (1.0 - BETA) * clip * update).astype(jnp.bfloat16)
    new_param = param - RATE * new_mom.astype(jnp.float32)
    return (new_param, new_mom, new_rows, new_cols, new_param.astype(jnp.bfloat16), jnp.log(row_mean), jnp.log(mean_square))

def reference(param_up, grad_up, mom_up, rows_up, cols_up, param_attn, grad_attn, mom_attn, rows_attn, cols_attn):
    p_up, m_up, r_up, c_up, k_up, l_up, s_up = adafactor(param_up, grad_up, mom_up, rows_up, cols_up)
    p_at, m_at, r_at, c_at, k_at, l_at, s_at = adafactor(param_attn, grad_attn, mom_attn, rows_attn, cols_attn)
    mean_logs = jnp.stack([l_up, l_at, s_up, s_at]).astype(jnp.float32)
    return (p_up, m_up, r_up, c_up, k_up, p_at, m_at, r_at, c_at, k_at, mean_logs)
```

```python
import functools

import jax
import jax.numpy as jnp
from jax import lax
from jax.experimental import pallas as pl
from jax.experimental.pallas import tpu as pltpu
from jax.sharding import PartitionSpec as P

DECAY = 0.8415
BETA = 0.9
RATE = 0.01
TINY = 1e-30

MESH = pl.DeviceIdType.MESH
F32 = jnp.float32
BF16 = jnp.bfloat16


def body(
    dims,
    p_up, g_up, m_up, r_up, c_up, p_at, g_at, m_at, r_at, c_at,
    np_up, nm_up, nr_up, nc_up, cp_up, np_at, nm_at, nr_at, nc_at, cp_at, logs,
    vg_up, vg_at, vm_up, vm_at, vp_up, vp_at, vr, vc,
    lane_part, rs, cs_y, cs_z, tt_y, tt_z, sq, in_sem,
    rs_send, rs_recv, cy_send, cy_recv, cz_send, cz_recv,
    ty_send, ty_recv, tz_send, tz_recv, sq_send, sq_recv,
    own_send, near_recv, far_send, far_recv, sib_send, sib_recv,
):
    ny, nz, nx = dims
    n_col = 2 * nx
    rows, cu = g_up.shape
    ca = g_at.shape[1]
    cw = cu + ca
    n_rows = rows * ny * nz
    full_up = cu * n_col
    full_at = ca * n_col

    row = lax.axis_index("row")
    col = lax.axis_index("col")
    y, z = row // nz, row % nz
    x, core = col // 2, col % 2

    col_peers = [lax.rem(col + k, n_col) for k in range(1, n_col)]
    y_peers = [lax.rem(y + k, ny) for k in range(1, ny)]
    z_peers = [lax.rem(z + k, nz) for k in range(1, nz)]

    barrier = pltpu.get_barrier_semaphore()
    for c in col_peers:
        pl.semaphore_signal(barrier, inc=1, device_id=(row, c), device_id_type=MESH)
    for q in y_peers:
        pl.semaphore_signal(barrier, inc=1, device_id=(q * nz + z, col), device_id_type=MESH)
    for q in z_peers:
        pl.semaphore_signal(barrier, inc=1, device_id=(y * nz + q, col), device_id_type=MESH)

    loads = [
        pltpu.make_async_copy(src, dst, in_sem.at[i])
        for i, (src, dst) in enumerate(
            [
                (g_up, vg_up),
                (g_at, vg_at),
                (r_up, vr.at[:, pl.ds(0, rows)]),
                (r_at, vr.at[:, pl.ds(rows, rows)]),
                (c_up, vc.at[:, pl.ds(0, cu)]),
                (c_at, vc.at[:, pl.ds(cu, ca)]),
                (m_up, vm_up),
                (p_up, vp_up),
                (m_at, vm_at),
                (p_at, vp_at),
            ]
        )
    ]
    for copy in loads:
        copy.start()

    loads[0].wait()
    loads[1].wait()
    step = 16
    acc = jnp.zeros((8, cw), F32)
    for r0 in range(0, rows, step):
        wide_u = vg_up[r0 : r0 + step, :].astype(F32)
        wide_a = vg_at[r0 : r0 + step, :].astype(F32)
        su = wide_u * wide_u + TINY
        sa = wide_a * wide_a + TINY
        both = jnp.concatenate([su, sa], axis=1)
        for s in range(0, step, 8):
            acc = acc + both[s : s + 8, :]
        lane_part[r0 : r0 + step, :] = functools.reduce(
            jnp.add, [su[:, k : k + 128] for k in range(0, cu, 128)]
        )
        lane_part[rows + r0 : rows + r0 + step, :] = functools.reduce(
            jnp.add, [sa[:, k : k + 128] for k in range(0, ca, 128)]
        )
    cs_y[y] = jnp.sum(acc, axis=0, keepdims=True)

    eye = lax.broadcasted_iota(jnp.int32, (rows, rows), 0) == lax.broadcasted_iota(
        jnp.int32, (rows, rows), 1
    )

    def to_lanes(column):
        return jnp.sum(jnp.where(eye, column, 0.0), axis=0, keepdims=True)

    def to_column(lanes):
        return jnp.sum(jnp.where(eye, lanes, 0.0), axis=1, keepdims=True)

    sums = jnp.sum(lane_part[...], axis=1, keepdims=True)
    rs[col] = jnp.concatenate([to_lanes(sums[:rows]), to_lanes(sums[rows:])], axis=1)

    pl.semaphore_wait(barrier, (n_col - 1) + (ny - 1) + (nz - 1))

    def spread(buf, slot, targets, peers, send, recv):
        out = []
        for k, (dev, peer) in enumerate(zip(targets, peers)):
            copy = pltpu.make_async_remote_copy(
                src_ref=buf.at[slot],
                dst_ref=buf.at[slot],
                send_sem=send.at[k],
                recv_sem=recv.at[slot],
                device_id=dev,
                device_id_type=MESH,
            )
            copy.start()
            out.append(copy)
        return out

    def arrive(buf, peers, recv, send):
        for peer in peers:
            pltpu.make_async_remote_copy(
                src_ref=buf.at[peer],
                dst_ref=buf.at[peer],
                send_sem=send.at[0],
                recv_sem=recv.at[peer],
                device_id=(row, col_peers[0]),
                device_id_type=MESH,
            ).wait_recv()

    def total(buf, n):
        return functools.reduce(jnp.add, [buf[k] for k in range(n)])

    col_devs = [(row, c) for c in col_peers]
    y_devs = [(q * nz + z, col) for q in y_peers]
    z_devs = [(y * nz + q, col) for q in z_peers]
    sent = []
    sent += spread(rs, col, col_devs, col_peers, rs_send, rs_recv)
    sent += spread(cs_y, y, y_devs, y_peers, cy_send, cy_recv)

    for k in range(2, 6):
        loads[k].wait()
    arrive(rs, col_peers, rs_recv, rs_send)
    full_rows = total(rs, n_col)
    old = vr[...]
    lane = lax.broadcasted_iota(jnp.int32, (1, 2 * rows), 1)
    width = jnp.where(lane < rows, 1.0 / full_up, 1.0 / full_at)
    new_rows = DECAY * old + (1.0 - DECAY) * (full_rows * width)
    nr_up[...] = new_rows[:, :rows]
    nr_at[...] = new_rows[:, rows:]
    nr_col_up = to_column(new_rows[:, :rows])
    nr_col_at = to_column(new_rows[:, rows:])
    inv_up = 1.0 / nr_col_up
    inv_at = 1.0 / nr_col_at

    acc = jnp.zeros((8, cw), F32)
    for r0 in range(0, rows, step):
        wide_u = vg_up[r0 : r0 + step, :].astype(F32)
        wide_a = vg_at[r0 : r0 + step, :].astype(F32)
        su = wide_u * wide_u * inv_up[r0 : r0 + step, :]
        sa = wide_a * wide_a * inv_at[r0 : r0 + step, :]
        both = jnp.concatenate([su, sa], axis=1)
        for s in range(0, step, 8):
            acc = acc + both[s : s + 8, :]
    tt_y[y] = jnp.concatenate([jnp.sum(acc, axis=0, keepdims=True), new_rows], axis=1)
    sent += spread(tt_y, y, y_devs, y_peers, ty_send, ty_recv)

    arrive(cs_y, y_peers, cy_recv, cy_send)
    cs_z[z] = total(cs_y, ny)
    sent += spread(cs_z, z, z_devs, z_peers, cz_send, cz_recv)

    arrive(tt_y, y_peers, ty_recv, ty_send)
    tt_z[z] = total(tt_y, ny)
    sent += spread(tt_z, z, z_devs, z_peers, tz_send, tz_recv)

    arrive(cs_z, z_peers, cz_recv, cz_send)
    new_cols = DECAY * vc[...] + (1.0 - DECAY) * (total(cs_z, nz) * (1.0 / n_rows))
    nc_up[...] = new_cols[:, :cu]
    nc_at[...] = new_cols[:, cu:]
    inv_cols = 1.0 / new_cols
    root_cols = lax.rsqrt(new_cols)
    root_up = lax.rsqrt(nr_col_up)
    root_at = lax.rsqrt(nr_col_at)

    arrive(tt_z, z_peers, tz_recv, tz_send)
    tt = total(tt_z, nz)
    terms = tt[:, :cw] * inv_cols
    fold = lambda v: functools.reduce(
        jnp.add, [v[:, k : k + 128] for k in range(0, v.shape[1], 128)]
    )
    sq[col] = jnp.concatenate([fold(terms[:, :cu]), fold(terms[:, cu:])], axis=1)
    sent += spread(sq, col, col_devs, col_peers, sq_send, sq_recv)
    mean_up = jnp.sum(tt[:, cw : cw + rows], axis=1, keepdims=True) * (1.0 / n_rows)
    mean_at = jnp.sum(tt[:, cw + rows :], axis=1, keepdims=True) * (1.0 / n_rows)
    for k in range(6, 10):
        loads[k].wait()

    arrive(sq, col_peers, sq_recv, sq_send)
    sums = total(sq, n_col)
    square_up = mean_up * (jnp.sum(sums[:, :128], axis=1, keepdims=True) * (1.0 / (n_rows * full_up)))
    square_at = mean_at * (jnp.sum(sums[:, 128:], axis=1, keepdims=True) * (1.0 / (n_rows * full_at)))
    clip_up = 1.0 / jnp.maximum(1.0, jnp.sqrt(square_up))
    clip_at = 1.0 / jnp.maximum(1.0, jnp.sqrt(square_at))
    cols_up = root_cols[:, :cu] * ((1.0 - BETA) * clip_up * jnp.sqrt(mean_up))
    cols_at = root_cols[:, cu:] * ((1.0 - BETA) * clip_at * jnp.sqrt(mean_at))

    off_up = pl.multiple_of(col * cu, cu)
    off_at = pl.multiple_of(col * ca, ca)

    def advance(up, r0, n):
        vg, vm, vp, new_p, new_m, copy_ref, root, cols, off, width = (
            (vg_up, vm_up, vp_up, np_up, nm_up, cp_up, root_up, cols_up, off_up, cu)
            if up
            else (vg_at, vm_at, vp_at, np_at, nm_at, cp_at, root_at, cols_at, off_at, ca)
        )
        for s in range(r0, r0 + n, 16):
            here = slice(s, s + 16)
            wide = vg[here, :].astype(F32)
            mom = (BETA * vm[here, :].astype(F32) + wide * root[here, :] * cols).astype(BF16)
            new_m[here, :] = mom
            param = vp[here, :] - RATE * mom.astype(F32)
            new_p[here, :] = param
            copy_ref[here, pl.ds(off, width)] = param.astype(BF16)

    n_u, n_a = 8, 2
    hu, ha = rows // n_u, rows // n_a
    pieces = [(True, k * hu, hu) for k in range(n_u)] + [(False, k * ha, ha) for k in range(n_a)]
    rightward = [0, 1, 2, 3, 8]
    leftward = [4, 5, 6, 7, 9]

    right = (row, lax.rem(x + 1, nx) * 2 + core)
    left = (row, lax.rem(x + nx - 1, nx) * 2 + core)
    across = lax.rem(x + 2, nx) * 2 + core
    sibling = (row, x * 2 + 1 - core)
    sib_col = x * 2 + 1 - core

    def view(piece, owner):
        up, r0, n = pieces[piece]
        if up:
            return cp_up.at[pl.ds(r0, n), pl.ds(pl.multiple_of(owner * cu, cu), cu)]
        return cp_at.at[pl.ds(r0, n), pl.ds(pl.multiple_of(owner * ca, ca), ca)]

    def block(up, owner):
        if up:
            return cp_up.at[:, pl.ds(pl.multiple_of(owner * cu, cu), cu)]
        return cp_at.at[:, pl.ds(pl.multiple_of(owner * ca, ca), ca)]

    def push(piece, owner, dev, send, recv):
        pltpu.make_async_remote_copy(
            src_ref=view(piece, owner),
            dst_ref=view(piece, owner),
            send_sem=send,
            recv_sem=recv,
            device_id=dev,
            device_id_type=MESH,
        ).start()

    def await_recv(ref, recv):
        pltpu.make_async_remote_copy(
            src_ref=ref, dst_ref=ref, send_sem=sib_send.at[0, 0], recv_sem=recv,
            device_id=sibling, device_id_type=MESH,
        ).wait_recv()

    def await_send(ref, send):
        pltpu.make_async_remote_copy(
            src_ref=ref, dst_ref=ref, send_sem=send, recv_sem=far_recv.at[0],
            device_id=sibling, device_id_type=MESH,
        ).wait_send()

    kind = lambda piece: 0 if pieces[piece][0] else 1
    order = [p for pair in zip(rightward, leftward) for p in pair]
    for p in order:
        advance(*pieces[p])
        first, second = (right, left) if p in rightward else (left, right)
        to_first, to_second = (0, 1) if p in rightward else (1, 0)
        push(p, col, first, own_send.at[to_first, kind(p)], near_recv.at[to_first, p])
        push(p, col, second, own_send.at[to_second, kind(p)], near_recv.at[to_second, p])
        push(p, col, sibling, sib_send.at[0, kind(p)], sib_recv.at[0, kind(p)])

    lane4 = lax.broadcasted_iota(jnp.int32, (1, 128), 1)
    four = jnp.where(
        lane4 == 0, mean_up, jnp.where(lane4 == 1, mean_at, jnp.where(lane4 == 2, square_up, square_at))
    )
    logs[...] = jnp.log(four)

    left_col, right_col = left[1], right[1]
    for a, b in zip(rightward, leftward):
        await_recv(view(a, left_col), near_recv.at[0, a])
        push(a, left_col, right, far_send.at[0, kind(a)], far_recv.at[a])
        push(a, left_col, sibling, sib_send.at[1, kind(a)], sib_recv.at[1, kind(a)])
        await_recv(view(b, right_col), near_recv.at[1, b])
        push(b, right_col, left, far_send.at[1, kind(b)], far_recv.at[b])
        push(b, right_col, sibling, sib_send.at[2, kind(b)], sib_recv.at[2, kind(b)])
    for a, b in zip(rightward, leftward):
        await_recv(view(b, left_col), near_recv.at[0, b])
        push(b, left_col, sibling, sib_send.at[1, kind(b)], sib_recv.at[1, kind(b)])
        await_recv(view(a, right_col), near_recv.at[1, a])
        push(a, right_col, sibling, sib_send.at[2, kind(a)], sib_recv.at[2, kind(a)])
        await_recv(view(a, across), far_recv.at[a])
        push(a, across, sibling, sib_send.at[3, kind(a)], sib_recv.at[3, kind(a)])
        await_recv(view(b, across), far_recv.at[b])
        push(b, across, sibling, sib_send.at[3, kind(b)], sib_recv.at[3, kind(b)])

    other = lambda c: c + 1 - 2 * core
    owners = [col, left_col, right_col, across]
    for k, owner in enumerate(owners):
        for t, up in enumerate((True, False)):
            await_recv(block(up, other(owner)), sib_recv.at[k, t])
            await_send(block(up, owner), sib_send.at[k, t])
    for side in range(2):
        for t, up in enumerate((True, False)):
            await_send(block(up, col), own_send.at[side, t])
            ref = cp_up if up else cp_at
            w = cu if up else ca
            await_send(
                ref.at[pl.ds(0, rows // 2), pl.ds(pl.multiple_of(col * w, w), w)],
                far_send.at[side, t],
            )
    for copy in sent:
        copy.wait_send()


def on_device(
    dims, p_up, g_up, m_up, r_up, c_up, p_at, g_at, m_at, r_at, c_at
):
    ny, nz, nx = dims
    n_col = 2 * nx
    rows, cu = g_up.shape
    ca = g_at.shape[1]
    cw = cu + ca
    dma = pltpu.SemaphoreType.DMA
    vm = pltpu.VMEM
    scratch = [
        vm((rows, cu), BF16), vm((rows, ca), BF16),
        vm((rows, cu), BF16), vm((rows, ca), BF16),
        vm((rows, cu), F32), vm((rows, ca), F32),
        vm((1, 2 * rows), F32), vm((1, cw), F32),
        vm((2 * rows, 128), F32),
        vm((n_col, 1, 2 * rows), F32),
        vm((ny, 1, cw), F32), vm((nz, 1, cw), F32),
        vm((ny, 1, cw + 2 * rows), F32), vm((nz, 1, cw + 2 * rows), F32),
        vm((n_col, 1, 256), F32),
        dma((10,)),
        dma((n_col - 1,)), dma((n_col,)),
        dma((max(ny - 1, 1),)), dma((ny,)),
        dma((max(nz - 1, 1),)), dma((nz,)),
        dma((max(ny - 1, 1),)), dma((ny,)),
        dma((max(nz - 1, 1),)), dma((nz,)),
        dma((n_col - 1,)), dma((n_col,)),
        dma((2, 2)), dma((2, 10)), dma((2, 2)), dma((10,)), dma((4, 2)), dma((4, 2)),
    ]
    out_shape = [
        vm((rows, cu), F32), vm((rows, cu), BF16), vm((1, rows), F32), vm((1, cu), F32),
        vm((rows, cu * n_col), BF16),
        vm((rows, ca), F32), vm((rows, ca), BF16), vm((1, rows), F32), vm((1, ca), F32),
        vm((rows, ca * n_col), BF16),
        vm((1, 128), F32),
    ]
    out_shape = [jax.ShapeDtypeStruct(o.shape, o.dtype) for o in out_shape]
    anywhere = pl.BlockSpec(memory_space=pltpu.HBM)
    inside = pl.BlockSpec(memory_space=pltpu.VMEM)
    (np_up, nm_up, nr_up, nc_up, cp_up, np_at, nm_at, nr_at, nc_at, cp_at, logs) = pl.pallas_call(
        functools.partial(body, dims),
        out_shape=out_shape,
        in_specs=[anywhere] * 10,
        out_specs=[inside] * 11,
        scratch_shapes=scratch,
        compiler_params=pltpu.CompilerParams(
            collective_id=0, has_side_effects=True, vmem_limit_bytes=40 * 1024 * 1024
        ),
        cost_estimate=pl.CostEstimate(
            flops=20 * rows * cw, bytes_accessed=10 * rows * cw, transcendentals=0
        ),
    )(
        *[
            pltpu.with_memory_space_constraint(a, pltpu.HBM)
            for a in (
                p_up, g_up, m_up, r_up.reshape(1, rows), c_up.reshape(1, cu),
                p_at, g_at, m_at, r_at.reshape(1, rows), c_at.reshape(1, ca),
            )
        ]
    )
    return (
        np_up, nm_up, nr_up.reshape(rows), nc_up.reshape(cu), cp_up,
        np_at, nm_at, nr_at.reshape(rows), nc_at.reshape(ca), cp_at,
        logs[0, :4],
    )


def solution(mesh, dims=(4, 8, 4)):
    block = P("row", "col")
    in_specs = (block, block, block, P("row"), P("col")) * 2
    out_specs = (block, block, P("row"), P("col"), P("row", None)) * 2 + (P(),)
    return jax.shard_map(
        functools.partial(on_device, dims),
        mesh=mesh,
        in_specs=in_specs,
        out_specs=out_specs,
        check_vma=False,
    )
```

```python
import functools

import jax
import jax.numpy as jnp
from jax import lax
from jax.experimental import pallas as pl
from jax.experimental.pallas import tpu as pltpu
from jax.sharding import PartitionSpec as P

DECAY = 0.8415
BETA = 0.9
RATE = 0.01
TINY = 1e-30

MESH = pl.DeviceIdType.MESH
F32 = jnp.float32
N_UP, N_AT = 8, 2
EARLY = 4
BF16 = jnp.bfloat16


def body(
    dims,
    p_up, g_up, m_up, r_up, c_up, p_at, g_at, m_at, r_at, c_at,
    np_up, nm_up, nr_up, nc_up, cp_up, np_at, nm_at, nr_at, nc_at, cp_at, logs,
    vg_up, vg_at, vm_up, vm_at, vp_up, vp_at, vr, vc,
    part_a, far_a, far_g, col_box,
    lane_part, rs, cs_y, cs_z, tt_y, tt_z, sq, in_sem,
    rs_send, rs_recv, cy_send, cy_recv, cz_send, cz_recv,
    ty_send, ty_recv, tz_send, tz_recv, sq_send, sq_recv,
    own_send, near_recv, far_send, far_recv, sib_send, sib_recv,
    early_send, early_recv, relay_send, relay_recv, box_send, box_recv,
):
    ny, nz, nx = dims
    n_col = 2 * nx
    rows, cu = g_up.shape
    ca = g_at.shape[1]
    cw = cu + ca
    n_rows = rows * ny * nz
    full_up = cu * n_col
    full_at = ca * n_col

    row = lax.axis_index("row")
    col = lax.axis_index("col")
    y, z = row // nz, row % nz
    x, core = col // 2, col % 2

    col_peers = [lax.rem(col + k, n_col) for k in range(1, n_col)]
    y_peers = [lax.rem(y + k, ny) for k in range(1, ny)]
    z_peers = [lax.rem(z + k, nz) for k in range(1, nz)]

    barrier = pltpu.get_barrier_semaphore()
    for c in col_peers:
        pl.semaphore_signal(barrier, inc=1, device_id=(row, c), device_id_type=MESH)
    for q in y_peers:
        pl.semaphore_signal(barrier, inc=1, device_id=(q * nz + z, col), device_id_type=MESH)
    for q in z_peers:
        pl.semaphore_signal(barrier, inc=1, device_id=(y * nz + q, col), device_id_type=MESH)

    loads = [
        pltpu.make_async_copy(src, dst, in_sem.at[i])
        for i, (src, dst) in enumerate(
            [
                (g_up, vg_up),
                (g_at, vg_at),
                (r_up, vr.at[:, pl.ds(0, rows)]),
                (r_at, vr.at[:, pl.ds(rows, rows)]),
                (c_up, vc.at[:, pl.ds(0, cu)]),
                (c_at, vc.at[:, pl.ds(cu, ca)]),
                (m_up, vm_up),
                (p_up, vp_up),
                (m_at, vm_at),
                (p_at, vp_at),
            ]
        )
    ]
    for copy in loads:
        copy.start()

    loads[0].wait()
    loads[1].wait()
    step = 16
    acc = jnp.zeros((8, cw), F32)
    for r0 in range(0, rows, step):
        wide_u = vg_up[r0 : r0 + step, :].astype(F32)
        wide_a = vg_at[r0 : r0 + step, :].astype(F32)
        su = wide_u * wide_u + TINY
        sa = wide_a * wide_a + TINY
        both = jnp.concatenate([su, sa], axis=1)
        for s in range(0, step, 8):
            acc = acc + both[s : s + 8, :]
        lane_part[r0 : r0 + step, :] = functools.reduce(
            jnp.add, [su[:, k : k + 128] for k in range(0, cu, 128)]
        )
        lane_part[rows + r0 : rows + r0 + step, :] = functools.reduce(
            jnp.add, [sa[:, k : k + 128] for k in range(0, ca, 128)]
        )
    cs_y[y] = jnp.sum(acc, axis=0, keepdims=True)

    eye = lax.broadcasted_iota(jnp.int32, (rows, rows), 0) == lax.broadcasted_iota(
        jnp.int32, (rows, rows), 1
    )

    def to_lanes(column):
        return jnp.sum(jnp.where(eye, column, 0.0), axis=0, keepdims=True)

    def to_column(lanes):
        return jnp.sum(jnp.where(eye, lanes, 0.0), axis=1, keepdims=True)

    sums = jnp.sum(lane_part[...], axis=1, keepdims=True)
    rs[col] = jnp.concatenate([to_lanes(sums[:rows]), to_lanes(sums[rows:])], axis=1)

    pl.semaphore_wait(barrier, (n_col - 1) + (ny - 1) + (nz - 1))

    def spread(buf, slot, targets, peers, send, recv):
        out = []
        for k, (dev, peer) in enumerate(zip(targets, peers)):
            copy = pltpu.make_async_remote_copy(
                src_ref=buf.at[slot],
                dst_ref=buf.at[slot],
                send_sem=send.at[k],
                recv_sem=recv.at[slot],
                device_id=dev,
                device_id_type=MESH,
            )
            copy.start()
            out.append(copy)
        return out

    def arrive(buf, peers, recv, send):
        for peer in peers:
            pltpu.make_async_remote_copy(
                src_ref=buf.at[peer],
                dst_ref=buf.at[peer],
                send_sem=send.at[0],
                recv_sem=recv.at[peer],
                device_id=(row, col_peers[0]),
                device_id_type=MESH,
            ).wait_recv()

    def total(buf, n):
        return functools.reduce(jnp.add, [buf[k] for k in range(n)])

    col_devs = [(row, c) for c in col_peers]
    y_devs = [(q * nz + z, col) for q in y_peers]
    z_devs = [(y * nz + q, col) for q in z_peers]
    sent = []
    sent += spread(rs, col, col_devs, col_peers, rs_send, rs_recv)
    sent += spread(cs_y, y, y_devs, y_peers, cy_send, cy_recv)

    hu, ha = rows // N_UP, rows // N_AT
    early_rows = EARLY * hu
    right = (row, lax.rem(x + 1, nx) * 2 + core)
    left = (row, lax.rem(x + nx - 1, nx) * 2 + core)
    across = lax.rem(x + 2, nx) * 2 + core
    sibling = (row, x * 2 + 1 - core)
    early_right = list(range(0, EARLY // 2))
    early_left = list(range(EARLY // 2, EARLY))
    early_order = [p for pair in zip(early_right, early_left) for p in pair]
    for k in range(6, 8):
        loads[k].wait()
    for p in range(EARLY):
        for r0 in range(p * hu, (p + 1) * hu, 16):
            here = slice(r0, r0 + 16)
            part_a[here, :] = (vp_up[here, :] - (RATE * BETA) * vm_up[here, :].astype(F32)).astype(BF16)

    def early_copy(p, which, src, dst, dev, send, recv):
        return pltpu.make_async_remote_copy(
            src_ref=src.at[pl.ds(p * hu, hu), :],
            dst_ref=dst.at[pl.ds(p * hu, hu), :],
            send_sem=send,
            recv_sem=recv,
            device_id=dev,
            device_id_type=MESH,
        )

    for p in early_order:
        sides = (0, 1) if p in early_right else (1, 0)
        for side in sides:
            for which, (src, box) in enumerate(((part_a, far_a), (vg_up, far_g))):
                copy = early_copy(
                    p, which, src, box.at[side], (right, left)[side],
                    early_send.at[side, p, which], early_recv.at[side, p, which],
                )
                copy.start()
                sent.append(copy)

    for k in range(2, 6):
        loads[k].wait()
    arrive(rs, col_peers, rs_recv, rs_send)
    full_rows = total(rs, n_col)
    old = vr[...]
    lane = lax.broadcasted_iota(jnp.int32, (1, 2 * rows), 1)
    width = jnp.where(lane < rows, 1.0 / full_up, 1.0 / full_at)
    new_rows = DECAY * old + (1.0 - DECAY) * (full_rows * width)
    nr_up[...] = new_rows[:, :rows]
    nr_at[...] = new_rows[:, rows:]
    nr_col_up = to_column(new_rows[:, :rows])
    nr_col_at = to_column(new_rows[:, rows:])
    inv_up = 1.0 / nr_col_up
    inv_at = 1.0 / nr_col_at

    acc = jnp.zeros((8, cw), F32)
    for r0 in range(0, rows, step):
        wide_u = vg_up[r0 : r0 + step, :].astype(F32)
        wide_a = vg_at[r0 : r0 + step, :].astype(F32)
        su = wide_u * wide_u * inv_up[r0 : r0 + step, :]
        sa = wide_a * wide_a * inv_at[r0 : r0 + step, :]
        both = jnp.concatenate([su, sa], axis=1)
        for s in range(0, step, 8):
            acc = acc + both[s : s + 8, :]
    tt_y[y] = jnp.concatenate([jnp.sum(acc, axis=0, keepdims=True), new_rows], axis=1)
    sent += spread(tt_y, y, y_devs, y_peers, ty_send, ty_recv)

    arrive(cs_y, y_peers, cy_recv, cy_send)
    cs_z[z] = total(cs_y, ny)
    sent += spread(cs_z, z, z_devs, z_peers, cz_send, cz_recv)

    arrive(tt_y, y_peers, ty_recv, ty_send)
    tt_z[z] = total(tt_y, ny)
    sent += spread(tt_z, z, z_devs, z_peers, tz_send, tz_recv)

    arrive(cs_z, z_peers, cz_recv, cz_send)
    new_cols = DECAY * vc[...] + (1.0 - DECAY) * (total(cs_z, nz) * (1.0 / n_rows))
    nc_up[...] = new_cols[:, :cu]
    nc_at[...] = new_cols[:, cu:]
    inv_cols = 1.0 / new_cols
    root_cols = lax.rsqrt(new_cols)
    root_up = lax.rsqrt(nr_col_up)
    root_at = lax.rsqrt(nr_col_at)
    x_devs = [(row, lax.rem(x + k, nx) * 2 + core) for k in range(1, nx)]
    if EARLY:
        col_box[0] = root_cols[:, :cu]
        for k in range(1, nx):
            copy = pltpu.make_async_remote_copy(
                src_ref=col_box.at[0], dst_ref=col_box.at[nx - k],
                send_sem=box_send.at[k], recv_sem=box_recv.at[nx - k],
                device_id=x_devs[k - 1], device_id_type=MESH,
            )
            copy.start()
            sent.append(copy)

    arrive(tt_z, z_peers, tz_recv, tz_send)
    tt = total(tt_z, nz)
    terms = tt[:, :cw] * inv_cols
    fold = lambda v: functools.reduce(
        jnp.add, [v[:, k : k + 128] for k in range(0, v.shape[1], 128)]
    )
    sq[col] = jnp.concatenate([fold(terms[:, :cu]), fold(terms[:, cu:])], axis=1)
    sent += spread(sq, col, col_devs, col_peers, sq_send, sq_recv)
    mean_up = jnp.sum(tt[:, cw : cw + rows], axis=1, keepdims=True) * (1.0 / n_rows)
    mean_at = jnp.sum(tt[:, cw + rows :], axis=1, keepdims=True) * (1.0 / n_rows)
    for k in range(8, 10):
        loads[k].wait()
    for p in early_order:
        side = 0 if p in early_right else 1
        for which, (src, box) in enumerate(((part_a, far_a), (vg_up, far_g))):
            early_copy(
                p, which, src, box.at[side], (right, left)[side],
                early_send.at[side, p, which], early_recv.at[side, p, which],
            ).wait_recv()
            copy = early_copy(
                p, which, box.at[side], box.at[2], (right, left)[side],
                relay_send.at[p, which], relay_recv.at[p, which],
            )
            copy.start()
            sent.append(copy)

    arrive(sq, col_peers, sq_recv, sq_send)
    sums = total(sq, n_col)
    square_up = mean_up * (jnp.sum(sums[:, :128], axis=1, keepdims=True) * (1.0 / (n_rows * full_up)))
    square_at = mean_at * (jnp.sum(sums[:, 128:], axis=1, keepdims=True) * (1.0 / (n_rows * full_at)))
    clip_up = 1.0 / jnp.maximum(1.0, jnp.sqrt(square_up))
    clip_at = 1.0 / jnp.maximum(1.0, jnp.sqrt(square_at))
    cols_up = root_cols[:, :cu] * ((1.0 - BETA) * clip_up * jnp.sqrt(mean_up))
    cols_at = root_cols[:, cu:] * ((1.0 - BETA) * clip_at * jnp.sqrt(mean_at))

    off_up = pl.multiple_of(col * cu, cu)
    off_at = pl.multiple_of(col * ca, ca)

    def advance(up, r0, n, early=False):
        vg, vm, vp, new_p, new_m, copy_ref, root, cols, off, width = (
            (vg_up, vm_up, vp_up, np_up, nm_up, cp_up, root_up, cols_up, off_up, cu)
            if up
            else (vg_at, vm_at, vp_at, np_at, nm_at, cp_at, root_at, cols_at, off_at, ca)
        )
        for s in range(r0, r0 + n, 16):
            here = slice(s, s + 16)
            wide = vg[here, :].astype(F32)
            mom = (BETA * vm[here, :].astype(F32) + wide * root[here, :] * cols).astype(BF16)
            new_m[here, :] = mom
            param = vp[here, :] - RATE * mom.astype(F32)
            new_p[here, :] = param
            if not early:
                copy_ref[here, pl.ds(off, width)] = param.astype(BF16)

    scale_up = RATE * (1.0 - BETA) * clip_up * jnp.sqrt(mean_up)

    def finish(a_ref, g_ref, roots, owner, p):
        scaled = roots * scale_up
        for r0 in range(p * hu, (p + 1) * hu, 16):
            here = slice(r0, r0 + 16)
            step = g_ref[here, :].astype(F32) * root_up[here, :] * scaled
            cp_up[here, pl.ds(pl.multiple_of(owner * cu, cu), cu)] = (
                a_ref[here, :].astype(F32) - step
            ).astype(BF16)

    pieces = [(True, k * hu, hu) for k in range(N_UP)] + [(False, k * ha, ha) for k in range(N_AT)]
    mid = (EARLY + N_UP) // 2
    rightward = list(range(EARLY, mid)) + [N_UP]
    leftward = list(range(mid, N_UP)) + [N_UP + 1]

    def view(piece, owner):
        up, r0, n = pieces[piece]
        if up:
            return cp_up.at[pl.ds(r0, n), pl.ds(pl.multiple_of(owner * cu, cu), cu)]
        return cp_at.at[pl.ds(r0, n), pl.ds(pl.multiple_of(owner * ca, ca), ca)]

    def block(up, owner):
        if up:
            return cp_up.at[:, pl.ds(pl.multiple_of(owner * cu, cu), cu)]
        return cp_at.at[:, pl.ds(pl.multiple_of(owner * ca, ca), ca)]

    def push(piece, owner, dev, send, recv):
        pltpu.make_async_remote_copy(
            src_ref=view(piece, owner),
            dst_ref=view(piece, owner),
            send_sem=send,
            recv_sem=recv,
            device_id=dev,
            device_id_type=MESH,
        ).start()

    def await_recv(ref, recv):
        pltpu.make_async_remote_copy(
            src_ref=ref, dst_ref=ref, send_sem=sib_send.at[0, 0], recv_sem=recv,
            device_id=sibling, device_id_type=MESH,
        ).wait_recv()

    def await_send(ref, send):
        pltpu.make_async_remote_copy(
            src_ref=ref, dst_ref=ref, send_sem=send, recv_sem=far_recv.at[0],
            device_id=sibling, device_id_type=MESH,
        ).wait_send()

    kind = lambda piece: 0 if pieces[piece][0] else 1
    order = [p for pair in zip(rightward, leftward) for p in pair]
    for p in order:
        advance(*pieces[p])
        first, second = (right, left) if p in rightward else (left, right)
        to_first, to_second = (0, 1) if p in rightward else (1, 0)
        push(p, col, first, own_send.at[to_first, kind(p)], near_recv.at[to_first, p])
        push(p, col, second, own_send.at[to_second, kind(p)], near_recv.at[to_second, p])
        push(p, col, sibling, sib_send.at[0, kind(p)], sib_recv.at[0, kind(p)])

    for p in range(EARLY):
        advance(*pieces[p], early=True)
        finish(part_a, vg_up, col_box[0], col, p)
        push(p, col, sibling, sib_send.at[0, 0], sib_recv.at[0, 0])

    lane4 = lax.broadcasted_iota(jnp.int32, (1, 128), 1)
    four = jnp.where(
        lane4 == 0, mean_up, jnp.where(lane4 == 1, mean_at, jnp.where(lane4 == 2, square_up, square_at))
    )
    logs[...] = jnp.log(four)[:, :4]

    left_col, right_col = left[1], right[1]
    if EARLY:
        for k in range(1, nx):
            pltpu.make_async_remote_copy(
                src_ref=col_box.at[0], dst_ref=col_box.at[k],
                send_sem=box_send.at[k], recv_sem=box_recv.at[k],
                device_id=x_devs[0], device_id_type=MESH,
            ).wait_recv()

    def finish_box(side, owner, box, p):
        if box == 2:
            for which, (src, arrived) in enumerate(((part_a, far_a), (vg_up, far_g))):
                early_copy(
                    p, which, src, arrived.at[2], right, relay_send.at[p, which], relay_recv.at[p, which]
                ).wait_recv()
        elif p not in (early_right, early_left)[box]:
            for which, (src, arrived) in enumerate(((part_a, far_a), (vg_up, far_g))):
                early_copy(
                    p, which, src, arrived.at[box], right,
                    early_send.at[box, p, which], early_recv.at[box, p, which],
                ).wait_recv()
        finish(far_a.at[box], far_g.at[box], col_box[side], owner, p)
        k = {0: 1, 1: 2, 2: 3}[box]
        push(p, owner, sibling, sib_send.at[k, 0], sib_recv.at[k, 0])

    for p in range(EARLY):
        finish_box(3, left_col, 0, p)
        finish_box(1, right_col, 1, p)
    for a, b in zip(rightward, leftward):
        await_recv(view(a, left_col), near_recv.at[0, a])
        push(a, left_col, right, far_send.at[0, kind(a)], far_recv.at[a])
        push(a, left_col, sibling, sib_send.at[1, kind(a)], sib_recv.at[1, kind(a)])
        await_recv(view(b, right_col), near_recv.at[1, b])
        push(b, right_col, left, far_send.at[1, kind(b)], far_recv.at[b])
        push(b, right_col, sibling, sib_send.at[2, kind(b)], sib_recv.at[2, kind(b)])
    for p in early_order:
        finish_box(2, across, 2, p)
    for a, b in zip(rightward, leftward):
        await_recv(view(b, left_col), near_recv.at[0, b])
        push(b, left_col, sibling, sib_send.at[1, kind(b)], sib_recv.at[1, kind(b)])
        await_recv(view(a, right_col), near_recv.at[1, a])
        push(a, right_col, sibling, sib_send.at[2, kind(a)], sib_recv.at[2, kind(a)])
        await_recv(view(a, across), far_recv.at[a])
        push(a, across, sibling, sib_send.at[3, kind(a)], sib_recv.at[3, kind(a)])
        await_recv(view(b, across), far_recv.at[b])
        push(b, across, sibling, sib_send.at[3, kind(b)], sib_recv.at[3, kind(b)])

    other = lambda c: c + 1 - 2 * core
    owners = [col, left_col, right_col, across]
    for k, owner in enumerate(owners):
        for t, up in enumerate((True, False)):
            await_recv(block(up, other(owner)), sib_recv.at[k, t])
            await_send(block(up, owner), sib_send.at[k, t])
    late = rows - early_rows
    for side in range(2):
        for t, (ref, n, w) in enumerate(((cp_up, late, cu), (cp_at, rows, ca))):
            here = pl.ds(pl.multiple_of(col * w, w), w)
            await_send(ref.at[pl.ds(0, n), here], own_send.at[side, t])
            await_send(ref.at[pl.ds(0, n // 2), here], far_send.at[side, t])
    for copy in sent:
        copy.wait_send()


def write_out(*refs):
    n = (len(refs) - 1) // 2
    sems = refs[-1]
    copies = [
        pltpu.make_async_copy(src, dst, sems.at[i])
        for i, (src, dst) in enumerate(zip(refs[:n], refs[n : 2 * n]))
    ]
    for copy in copies:
        copy.start()
    for copy in copies:
        copy.wait()


def on_device(
    dims, p_up, g_up, m_up, r_up, c_up, p_at, g_at, m_at, r_at, c_at
):
    ny, nz, nx = dims
    n_col = 2 * nx
    rows, cu = g_up.shape
    ca = g_at.shape[1]
    cw = cu + ca
    n_early = max(EARLY, 1)
    early = n_early * (rows // N_UP)
    dma = pltpu.SemaphoreType.DMA
    vm = pltpu.VMEM
    scratch = [
        vm((rows, cu), BF16), vm((rows, ca), BF16),
        vm((rows, cu), BF16), vm((rows, ca), BF16),
        vm((rows, cu), F32), vm((rows, ca), F32),
        vm((1, 2 * rows), F32), vm((1, cw), F32),
        vm((early, cu), BF16), vm((3, early, cu), BF16), vm((3, early, cu), BF16), vm((nx, 1, cu), F32),
        vm((2 * rows, 128), F32),
        vm((n_col, 1, 2 * rows), F32),
        vm((ny, 1, cw), F32), vm((nz, 1, cw), F32),
        vm((ny, 1, cw + 2 * rows), F32), vm((nz, 1, cw + 2 * rows), F32),
        vm((n_col, 1, 256), F32),
        dma((10,)),
        dma((n_col - 1,)), dma((n_col,)),
        dma((max(ny - 1, 1),)), dma((ny,)),
        dma((max(nz - 1, 1),)), dma((nz,)),
        dma((max(ny - 1, 1),)), dma((ny,)),
        dma((max(nz - 1, 1),)), dma((nz,)),
        dma((n_col - 1,)), dma((n_col,)),
        dma((2, 2)), dma((2, 10)), dma((2, 2)), dma((10,)), dma((4, 2)), dma((4, 2)),
        dma((2, n_early, 2)), dma((2, n_early, 2)), dma((n_early, 2)), dma((n_early, 2)),
        dma((nx,)), dma((nx,)),
    ]
    out_shape = [
        vm((rows, cu), F32), vm((rows, cu), BF16), vm((1, rows), F32), vm((1, cu), F32),
        vm((rows, cu * n_col), BF16),
        vm((rows, ca), F32), vm((rows, ca), BF16), vm((1, rows), F32), vm((1, ca), F32),
        vm((rows, ca * n_col), BF16),
        vm((1, 4), F32),
    ]
    anywhere = pl.BlockSpec(memory_space=pltpu.HBM)
    inside = pl.BlockSpec(memory_space=pltpu.VMEM)
    results = pl.pallas_call(
        functools.partial(body, dims),
        out_shape=out_shape,
        in_specs=[anywhere] * 10,
        out_specs=[inside] * 11,
        scratch_shapes=scratch,
        compiler_params=pltpu.CompilerParams(
            collective_id=0, has_side_effects=True, vmem_limit_bytes=40 * 1024 * 1024
        ),
        cost_estimate=pl.CostEstimate(
            flops=20 * rows * cw, bytes_accessed=10 * rows * cw, transcendentals=0
        ),
    )(
        *[
            pltpu.with_memory_space_constraint(a, pltpu.HBM)
            for a in (
                p_up, g_up, m_up, r_up.reshape(1, rows), c_up.reshape(1, cu),
                p_at, g_at, m_at, r_at.reshape(1, rows), c_at.reshape(1, ca),
            )
        ]
    )
    (np_up, nm_up, nr_up, nc_up, cp_up, np_at, nm_at, nr_at, nc_at, cp_at, logs) = pl.pallas_call(
        write_out,
        out_shape=[pltpu.HBM(o.shape, o.dtype) for o in out_shape],
        in_specs=[inside] * 11,
        out_specs=[anywhere] * 11,
        scratch_shapes=[dma((11,))],
        compiler_params=pltpu.CompilerParams(vmem_limit_bytes=1024 * 1024),
        cost_estimate=pl.CostEstimate(
            flops=0, bytes_accessed=2 * rows * cw * (n_col + 3), transcendentals=0
        ),
    )(*[pltpu.with_memory_space_constraint(r, pltpu.VMEM) for r in results])
    return (
        np_up, nm_up, nr_up.reshape(rows), nc_up.reshape(cu), cp_up,
        np_at, nm_at, nr_at.reshape(rows), nc_at.reshape(ca), cp_at,
        logs.reshape(4),
    )


def solution(mesh, dims=(4, 8, 4)):
    block = P("row", "col")
    in_specs = (block, block, block, P("row"), P("col")) * 2
    out_specs = (block, block, P("row"), P("col"), P("row", None)) * 2 + (P(),)
    return jax.shard_map(
        functools.partial(on_device, dims),
        mesh=mesh,
        in_specs=in_specs,
        out_specs=out_specs,
        check_vma=False,
    )
```

```python
import functools

import jax
import jax.numpy as jnp
from jax import lax
from jax.experimental import pallas as pl
from jax.experimental.pallas import tpu as pltpu
from jax.sharding import PartitionSpec as P

DECAY = 0.8415
BETA = 0.9
RATE = 0.01
TINY = 1e-30

MESH = pl.DeviceIdType.MESH
F32 = jnp.float32
STEP = 16
EARLY = 80
BF16 = jnp.bfloat16


def body(
    dims,
    p_up, g_up, m_up, r_up, c_up, p_at, g_at, m_at, r_at, c_at,
    np_up, nm_up, nr_up, nc_up, cp_up, np_at, nm_at, nr_at, nc_at, cp_at, logs,
    vg_up, vg_at, vm_up, vm_at, vp_up, vp_at, vr, vc,
    part_a, far_a, far_g, col_box,
    lane_part, rs, cs_y, cs_z, tt_y, tt_z, sq, in_sem,
    rs_send, rs_recv, cy_send, cy_recv, cz_send, cz_recv,
    ty_send, ty_recv, tz_send, tz_recv, sq_send, sq_recv,
    own_send, near_recv, far_send, far_recv, sib_send, sib_recv,
    wave_send, wave_recv, box_send, box_recv, row_ready, ring_ready,
):
    ny, nz, nx = dims
    n_col = 2 * nx
    rows, cu = g_up.shape
    ca = g_at.shape[1]
    cw = cu + ca
    n_rows = rows * ny * nz
    full_up = cu * n_col
    full_at = ca * n_col

    row = lax.axis_index("row")
    col = lax.axis_index("col")
    y, z = row // nz, row % nz
    x, core = col // 2, col % 2

    col_peers = [lax.rem(col + k, n_col) for k in range(1, n_col)]
    y_peers = [lax.rem(y + k, ny) for k in range(1, ny)]
    z_peers = [lax.rem(z + k, nz) for k in sorted(range(1, nz), key=lambda k: -min(k, nz - k))]

    barrier = pltpu.get_barrier_semaphore()
    sib = (row, x * 2 + 1 - core)
    for k in range(1, nx):
        there = (row, lax.rem(x + k, nx) * 2)
        pl.semaphore_signal(barrier, inc=1, device_id=there, device_id_type=MESH)
    pl.when(core == 1)(
        lambda: pl.semaphore_signal(barrier, inc=1, device_id=sib, device_id_type=MESH)
    )
    for q in [y * nz + q for q in z_peers] + [q * nz + z for q in y_peers]:
        pl.semaphore_signal(barrier, inc=1, device_id=(q, x * 2 + 1), device_id_type=MESH)

    loads = [
        pltpu.make_async_copy(src, dst, in_sem.at[i])
        for i, (src, dst) in enumerate(
            [
                (g_up, vg_up),
                (g_at, vg_at),
                (r_up, vr.at[:, pl.ds(0, rows)]),
                (r_at, vr.at[:, pl.ds(rows, rows)]),
                (c_up, vc.at[:, pl.ds(0, cu)]),
                (c_at, vc.at[:, pl.ds(cu, ca)]),
                (m_up, vm_up),
                (p_up, vp_up),
                (m_at, vm_at),
                (p_at, vp_at),
            ]
        )
    ]
    for copy in loads:
        copy.start()

    loads[0].wait()
    loads[1].wait()
    step = 16
    acc = jnp.zeros((8, cw), F32)
    for r0 in range(0, rows, step):
        wide_u = vg_up[r0 : r0 + step, :].astype(F32)
        wide_a = vg_at[r0 : r0 + step, :].astype(F32)
        su = wide_u * wide_u + TINY
        sa = wide_a * wide_a + TINY
        both = jnp.concatenate([su, sa], axis=1)
        for s in range(0, step, 8):
            acc = acc + both[s : s + 8, :]
        lane_part[r0 : r0 + step, :] = functools.reduce(
            jnp.add, [su[:, k : k + 128] for k in range(0, cu, 128)]
        )
        lane_part[rows + r0 : rows + r0 + step, :] = functools.reduce(
            jnp.add, [sa[:, k : k + 128] for k in range(0, ca, 128)]
        )
    cs_y[y] = jnp.sum(acc, axis=0, keepdims=True)

    eye = lax.broadcasted_iota(jnp.int32, (rows, rows), 0) == lax.broadcasted_iota(
        jnp.int32, (rows, rows), 1
    )

    def to_lanes(column):
        return jnp.sum(jnp.where(eye, column, 0.0), axis=0, keepdims=True)

    def to_column(lanes):
        return jnp.sum(jnp.where(eye, lanes, 0.0), axis=1, keepdims=True)

    sums = jnp.sum(lane_part[...], axis=1, keepdims=True)
    rs[col] = jnp.concatenate([to_lanes(sums[:rows]), to_lanes(sums[rows:])], axis=1)

    for k in range(6, 8):
        loads[k].wait()
    for r0 in range(0, EARLY, 16):
        here = slice(r0, r0 + 16)
        part_a[here, :] = (vp_up[here, :] - (RATE * BETA) * vm_up[here, :].astype(F32)).astype(BF16)

    @pl.when(core == 0)
    def _():
        pl.semaphore_wait(barrier, n_col - 1)
        pl.semaphore_signal(row_ready, inc=1, device_id=sib, device_id_type=MESH)

    @pl.when(core == 1)
    def _():
        pl.semaphore_wait(row_ready, 1)

    def spread(buf, slot, targets, peers, send, recv):
        out = []
        for k, (dev, peer) in enumerate(zip(targets, peers)):
            copy = pltpu.make_async_remote_copy(
                src_ref=buf.at[slot],
                dst_ref=buf.at[slot],
                send_sem=send.at[k],
                recv_sem=recv.at[slot],
                device_id=dev,
                device_id_type=MESH,
            )
            copy.start()
            out.append(copy)
        return out

    def arrive(buf, peers, recv, send):
        for peer in peers:
            pltpu.make_async_remote_copy(
                src_ref=buf.at[peer],
                dst_ref=buf.at[peer],
                send_sem=send.at[0],
                recv_sem=recv.at[peer],
                device_id=(row, col_peers[0]),
                device_id_type=MESH,
            ).wait_recv()

    def total(buf, n):
        return functools.reduce(jnp.add, [buf[k] for k in range(n)])

    col_devs = [(row, c) for c in col_peers]
    y_devs = [(q * nz + z, col) for q in y_peers]
    z_devs = [(y * nz + q, col) for q in z_peers]
    sent = []
    sent += spread(rs, col, col_devs, col_peers, rs_send, rs_recv)

    right = (row, lax.rem(x + 1, nx) * 2 + core)
    left = (row, lax.rem(x + nx - 1, nx) * 2 + core)
    across = lax.rem(x + 2, nx) * 2 + core
    sibling = (row, x * 2 + 1 - core)
    ways = (right, left)
    half = cu // 2

    def early_copy(wave, way, which, part, box):
        src = ((part_a, vg_up) if wave != 1 else (far_a.at[way], far_g.at[way]))[which]
        dst = (far_a, far_g)[which].at[box]
        rows_, cols_ = pl.ds(0, EARLY), pl.ds(part * half, half)
        return pltpu.make_async_remote_copy(
            src_ref=src.at[rows_, cols_],
            dst_ref=dst.at[rows_, cols_],
            send_sem=wave_send.at[wave, way, which],
            recv_sem=wave_recv.at[wave, way, which],
            device_id=ways[way],
            device_id_type=MESH,
        )

    def early_args(wave, way):
        return (way, (way, 2, way)[wave]) if wave < 2 else (1 - way, way)

    def start_wave(wave, parts=(0, 1)):
        for way in range(2):
            for which in parts:
                copy = early_copy(wave, way, which, *early_args(wave, way))
                copy.start()
                sent.append(copy)

    def await_wave(wave, way, parts=(0, 1)):
        for which in parts:
            early_copy(wave, way, which, *early_args(wave, way)).wait_recv()

    start_wave(0)
    start_wave(2)

    @pl.when(core == 1)
    def _():
        pl.semaphore_wait(barrier, 2 * ((ny - 1) + (nz - 1)))
        pl.semaphore_signal(ring_ready, inc=1, device_id=sib, device_id_type=MESH)

    @pl.when(core == 0)
    def _():
        pl.semaphore_wait(ring_ready, 1)

    sent += spread(cs_y, y, y_devs, y_peers, cy_send, cy_recv)

    for k in range(2, 6):
        loads[k].wait()
    arrive(rs, col_peers, rs_recv, rs_send)
    full_rows = total(rs, n_col)
    old = vr[...]
    lane = lax.broadcasted_iota(jnp.int32, (1, 2 * rows), 1)
    width = jnp.where(lane < rows, 1.0 / full_up, 1.0 / full_at)
    new_rows = DECAY * old + (1.0 - DECAY) * (full_rows * width)
    nr_up[...] = new_rows[:, :rows]
    nr_at[...] = new_rows[:, rows:]
    nr_col_up = to_column(new_rows[:, :rows])
    nr_col_at = to_column(new_rows[:, rows:])
    inv_up = 1.0 / nr_col_up
    inv_at = 1.0 / nr_col_at

    acc = jnp.zeros((8, cw), F32)
    for r0 in range(0, rows, step):
        wide_u = vg_up[r0 : r0 + step, :].astype(F32)
        wide_a = vg_at[r0 : r0 + step, :].astype(F32)
        su = wide_u * wide_u * inv_up[r0 : r0 + step, :]
        sa = wide_a * wide_a * inv_at[r0 : r0 + step, :]
        both = jnp.concatenate([su, sa], axis=1)
        for s in range(0, step, 8):
            acc = acc + both[s : s + 8, :]
    tt_y[y] = jnp.concatenate([jnp.sum(acc, axis=0, keepdims=True), new_rows], axis=1)
    sent += spread(tt_y, y, y_devs, y_peers, ty_send, ty_recv)

    arrive(cs_y, y_peers, cy_recv, cy_send)
    cs_z[z] = total(cs_y, ny)
    sent += spread(cs_z, z, z_devs, z_peers, cz_send, cz_recv)

    arrive(tt_y, y_peers, ty_recv, ty_send)
    tt_z[z] = total(tt_y, ny)
    sent += spread(tt_z, z, z_devs, z_peers, tz_send, tz_recv)


    arrive(cs_z, z_peers, cz_recv, cz_send)
    new_cols = DECAY * vc[...] + (1.0 - DECAY) * (total(cs_z, nz) * (1.0 / n_rows))
    nc_up[...] = new_cols[:, :cu]
    nc_at[...] = new_cols[:, cu:]
    inv_cols = 1.0 / new_cols
    root_cols = lax.rsqrt(new_cols)
    root_up = lax.rsqrt(nr_col_up)
    root_at = lax.rsqrt(nr_col_at)
    x_devs = [(row, lax.rem(x + k, nx) * 2 + core) for k in range(1, nx)]
    if True:
        col_box[0] = root_cols[:, :cu]
        for k in range(1, nx):
            copy = pltpu.make_async_remote_copy(
                src_ref=col_box.at[0], dst_ref=col_box.at[nx - k],
                send_sem=box_send.at[k], recv_sem=box_recv.at[nx - k],
                device_id=x_devs[k - 1], device_id_type=MESH,
            )
            copy.start()
            sent.append(copy)

    for way in range(2):
        await_wave(0, way, (0,))
    start_wave(1, (0,))
    arrive(tt_z, z_peers, tz_recv, tz_send)
    tt = total(tt_z, nz)
    terms = tt[:, :cw] * inv_cols
    fold = lambda v: functools.reduce(
        jnp.add, [v[:, k : k + 128] for k in range(0, v.shape[1], 128)]
    )
    sq[col] = jnp.concatenate([fold(terms[:, :cu]), fold(terms[:, cu:])], axis=1)
    sent += spread(sq, col, col_devs, col_peers, sq_send, sq_recv)
    mean_up = jnp.sum(tt[:, cw : cw + rows], axis=1, keepdims=True) * (1.0 / n_rows)
    mean_at = jnp.sum(tt[:, cw + rows :], axis=1, keepdims=True) * (1.0 / n_rows)
    for k in range(8, 10):
        loads[k].wait()
    for way in range(2):
        await_wave(0, way, (1,))
    start_wave(1, (1,))
    arrive(sq, col_peers, sq_recv, sq_send)
    sums = total(sq, n_col)
    square_up = mean_up * (jnp.sum(sums[:, :128], axis=1, keepdims=True) * (1.0 / (n_rows * full_up)))
    square_at = mean_at * (jnp.sum(sums[:, 128:], axis=1, keepdims=True) * (1.0 / (n_rows * full_at)))
    clip_up = 1.0 / jnp.maximum(1.0, jnp.sqrt(square_up))
    clip_at = 1.0 / jnp.maximum(1.0, jnp.sqrt(square_at))
    cols_up = root_cols[:, :cu] * ((1.0 - BETA) * clip_up * jnp.sqrt(mean_up))
    cols_at = root_cols[:, cu:] * ((1.0 - BETA) * clip_at * jnp.sqrt(mean_at))

    off_up = pl.multiple_of(col * cu, cu)
    off_at = pl.multiple_of(col * ca, ca)

    def advance(up, r0, n, early=False):
        vg, vm, vp, new_p, new_m, copy_ref, root, cols, off, width = (
            (vg_up, vm_up, vp_up, np_up, nm_up, cp_up, root_up, cols_up, off_up, cu)
            if up
            else (vg_at, vm_at, vp_at, np_at, nm_at, cp_at, root_at, cols_at, off_at, ca)
        )
        for s in range(r0, r0 + n, 16):
            here = slice(s, s + 16)
            wide = vg[here, :].astype(F32)
            mom = (BETA * vm[here, :].astype(F32) + wide * root[here, :] * cols).astype(BF16)
            new_m[here, :] = mom
            param = vp[here, :] - RATE * mom.astype(F32)
            new_p[here, :] = param
            if not early:
                copy_ref[here, pl.ds(off, width)] = param.astype(BF16)

    scale_up = RATE * (1.0 - BETA) * clip_up * jnp.sqrt(mean_up)

    def finish(a_ref, g_ref, roots, owner):
        scaled = roots * scale_up
        for r0 in range(0, EARLY, 16):
            here = slice(r0, r0 + 16)
            move = g_ref[here, :].astype(F32) * root_up[here, :] * scaled
            cp_up[here, pl.ds(pl.multiple_of(owner * cu, cu), cu)] = (
                a_ref[here, :].astype(F32) - move
            ).astype(BF16)

    quarter = rows // 4
    units = [[], []]
    chunks = []
    for r0 in range(EARLY, rows, STEP):
        chunks.append([(True, r0, STEP)])
        for way in range(2):
            units[way].append((True, r0, STEP, way * half, half))
    for k in range(2):
        chunks.append([(False, (2 * way + k) * quarter, quarter) for way in range(2)])
        for way in range(2):
            units[way].append((False, (2 * way + k) * quarter, quarter, 0, ca))
    n_late = len(chunks)

    def view(unit, owner):
        up, r0, n, c0, w = unit
        ref, width = (cp_up, cu) if up else (cp_at, ca)
        return ref.at[pl.ds(r0, n), pl.ds(pl.multiple_of(owner * width + c0, w), w)]

    def block(up, owner):
        if up:
            return cp_up.at[:, pl.ds(pl.multiple_of(owner * cu, cu), cu)]
        return cp_at.at[:, pl.ds(pl.multiple_of(owner * ca, ca), ca)]

    def push(piece, owner, dev, send, recv):
        pltpu.make_async_remote_copy(
            src_ref=view(piece, owner),
            dst_ref=view(piece, owner),
            send_sem=send,
            recv_sem=recv,
            device_id=dev,
            device_id_type=MESH,
        ).start()

    def await_recv(ref, recv):
        pltpu.make_async_remote_copy(
            src_ref=ref, dst_ref=ref, send_sem=sib_send.at[0, 0], recv_sem=recv,
            device_id=sibling, device_id_type=MESH,
        ).wait_recv()

    def await_send(ref, send):
        pltpu.make_async_remote_copy(
            src_ref=ref, dst_ref=ref, send_sem=send, recv_sem=far_recv.at[0, 0],
            device_id=sibling, device_id_type=MESH,
        ).wait_send()

    kind = lambda unit: 0 if unit[0] else 1

    def to_sibling(unit, owner, k):
        push(unit, owner, sibling, sib_send.at[k, kind(unit)], sib_recv.at[k, kind(unit)])

    def near(way, part, i):
        unit = units[part][i]
        push(unit, col, ways[way], own_send.at[way, kind(unit)], near_recv.at[way, part, i])

    for i in range(n_late):
        for up, r0, n in chunks[i]:
            advance(up, r0, n)
        near(0, 0, i)
        near(1, 1, i)
        for up, r0, n in chunks[i]:
            to_sibling((up, r0, n, 0, cu if up else ca), col, 0)
    advance(True, 0, EARLY, early=True)
    finish(part_a, vg_up, col_box[0], col)
    to_sibling((True, 0, EARLY, 0, cu), col, 0)

    lane4 = lax.broadcasted_iota(jnp.int32, (1, 128), 1)
    four = jnp.where(
        lane4 == 0, mean_up, jnp.where(lane4 == 1, mean_at, jnp.where(lane4 == 2, square_up, square_at))
    )
    logs[...] = jnp.log(four)[:, :4]

    left_col, right_col = left[1], right[1]
    if EARLY:
        for k in range(1, nx):
            pltpu.make_async_remote_copy(
                src_ref=col_box.at[0], dst_ref=col_box.at[k],
                send_sem=box_send.at[k], recv_sem=box_recv.at[k],
                device_id=x_devs[0], device_id_type=MESH,
            ).wait_recv()

    def finish_box(box):
        owner, column, waves = (
            (left_col, 3, ((0, 0), (2, 0))), (right_col, 1, ((0, 1), (2, 1))), (across, 2, ((1, 0), (1, 1)))
        )[box]
        for wave, way in waves:
            if wave:
                await_wave(wave, way)
        finish(far_a.at[box], far_g.at[box], col_box[column], owner)
        to_sibling((True, 0, EARLY, 0, cu), owner, box + 1)

    from_cols = (left_col, right_col)
    for i in range(n_late):
        if i < 3:
            finish_box((2, 0, 1)[i])
        for way in range(2):
            unit, owner = units[way][i], from_cols[way]
            await_recv(view(unit, owner), near_recv.at[way, way, i])
            push(unit, owner, ways[way], far_send.at[way, kind(unit)], far_recv.at[way, i])
            near(way, 1 - way, i)
            to_sibling(unit, owner, way + 1)
    for copy in sent:
        copy.wait_send()
    for i in range(n_late):
        for way in range(2):
            unit = units[way][i]
            await_recv(view(unit, across), far_recv.at[way, i])
            to_sibling(unit, across, 3)
        for way in range(2):
            unit = units[1 - way][i]
            await_recv(view(unit, from_cols[way]), near_recv.at[way, 1 - way, i])
            to_sibling(unit, from_cols[way], way + 1)

    late = rows - EARLY
    for side in range(2):
        for t, (ref, n, w) in enumerate(((cp_up, late, cu), (cp_at, rows, ca))):
            here = pl.ds(pl.multiple_of(col * w, w), w)
            await_send(ref.at[pl.ds(0, n), here], own_send.at[side, t])
            here = pl.ds(pl.multiple_of(col * w, w // 2), w // 2)
            await_send(ref.at[pl.ds(0, n), here], far_send.at[side, t])
    other = lambda c: c + 1 - 2 * core
    owners = [col, left_col, right_col, across]
    for k, owner in enumerate(owners):
        for t, up in enumerate((True, False)):
            await_send(block(up, owner), sib_send.at[k, t])
            await_recv(block(up, other(owner)), sib_recv.at[k, t])


def write_out(*refs):
    n = (len(refs) - 1) // 2
    sems = refs[-1]
    copies = [
        pltpu.make_async_copy(src, dst, sems.at[i])
        for i, (src, dst) in enumerate(zip(refs[:n], refs[n : 2 * n]))
    ]
    for copy in copies:
        copy.start()
    for copy in copies:
        copy.wait()


def on_device(
    dims, p_up, g_up, m_up, r_up, c_up, p_at, g_at, m_at, r_at, c_at
):
    ny, nz, nx = dims
    n_col = 2 * nx
    rows, cu = g_up.shape
    ca = g_at.shape[1]
    cw = cu + ca
    n_late = (rows - EARLY) // STEP + 2
    dma = pltpu.SemaphoreType.DMA
    vm = pltpu.VMEM
    scratch = [
        vm((rows, cu), BF16), vm((rows, ca), BF16),
        vm((rows, cu), BF16), vm((rows, ca), BF16),
        vm((rows, cu), F32), vm((rows, ca), F32),
        vm((1, 2 * rows), F32), vm((1, cw), F32),
        vm((EARLY, cu), BF16), vm((3, EARLY, cu), BF16), vm((3, EARLY, cu), BF16), vm((nx, 1, cu), F32),
        vm((2 * rows, 128), F32),
        vm((n_col, 1, 2 * rows), F32),
        vm((ny, 1, cw), F32), vm((nz, 1, cw), F32),
        vm((ny, 1, cw + 2 * rows), F32), vm((nz, 1, cw + 2 * rows), F32),
        vm((n_col, 1, 256), F32),
        dma((10,)),
        dma((n_col - 1,)), dma((n_col,)),
        dma((max(ny - 1, 1),)), dma((ny,)),
        dma((max(nz - 1, 1),)), dma((nz,)),
        dma((max(ny - 1, 1),)), dma((ny,)),
        dma((max(nz - 1, 1),)), dma((nz,)),
        dma((n_col - 1,)), dma((n_col,)),
        dma((2, 2)), dma((2, 2, n_late)), dma((2, 2)), dma((2, n_late)), dma((4, 2)), dma((4, 2)),
        dma((3, 2, 2)), dma((3, 2, 2)),
        dma((nx,)), dma((nx,)),
        pltpu.SemaphoreType.REGULAR, pltpu.SemaphoreType.REGULAR,
    ]
    out_shape = [
        vm((rows, cu), F32), vm((rows, cu), BF16), vm((1, rows), F32), vm((1, cu), F32),
        vm((rows, cu * n_col), BF16),
        vm((rows, ca), F32), vm((rows, ca), BF16), vm((1, rows), F32), vm((1, ca), F32),
        vm((rows, ca * n_col), BF16),
        vm((1, 4), F32),
    ]
    anywhere = pl.BlockSpec(memory_space=pltpu.HBM)
    inside = pl.BlockSpec(memory_space=pltpu.VMEM)
    results = pl.pallas_call(
        functools.partial(body, dims),
        out_shape=out_shape,
        in_specs=[anywhere] * 10,
        out_specs=[inside] * 11,
        scratch_shapes=scratch,
        compiler_params=pltpu.CompilerParams(
            collective_id=0, has_side_effects=True, vmem_limit_bytes=40 * 1024 * 1024
        ),
        cost_estimate=pl.CostEstimate(
            flops=20 * rows * cw, bytes_accessed=10 * rows * cw, transcendentals=0
        ),
    )(
        *[
            pltpu.with_memory_space_constraint(a, pltpu.HBM)
            for a in (
                p_up, g_up, m_up, r_up.reshape(1, rows), c_up.reshape(1, cu),
                p_at, g_at, m_at, r_at.reshape(1, rows), c_at.reshape(1, ca),
            )
        ]
    )
    (np_up, nm_up, nr_up, nc_up, cp_up, np_at, nm_at, nr_at, nc_at, cp_at, logs) = pl.pallas_call(
        write_out,
        out_shape=[pltpu.HBM(o.shape, o.dtype) for o in out_shape],
        in_specs=[inside] * 11,
        out_specs=[anywhere] * 11,
        scratch_shapes=[dma((11,))],
        compiler_params=pltpu.CompilerParams(vmem_limit_bytes=1024 * 1024),
        cost_estimate=pl.CostEstimate(
            flops=0, bytes_accessed=2 * rows * cw * (n_col + 3), transcendentals=0
        ),
    )(*[pltpu.with_memory_space_constraint(r, pltpu.VMEM) for r in results])
    return (
        np_up, nm_up, nr_up.reshape(rows), nc_up.reshape(cu), cp_up,
        np_at, nm_at, nr_at.reshape(rows), nc_at.reshape(ca), cp_at,
        logs.reshape(4),
    )


def solution(mesh, dims=(4, 8, 4)):
    block = P("row", "col")
    in_specs = (block, block, block, P("row"), P("col")) * 2
    out_specs = (block, block, P("row"), P("col"), P("row", None)) * 2 + (P(),)
    return jax.shard_map(
        functools.partial(on_device, dims),
        mesh=mesh,
        in_specs=in_specs,
        out_specs=out_specs,
        check_vma=False,
    )
```

```python
import functools

import jax
import jax.numpy as jnp
from jax import lax
from jax.experimental import pallas as pl
from jax.experimental.pallas import tpu as pltpu
from jax.sharding import PartitionSpec as P

DECAY = 0.8415
BETA = 0.9
RATE = 0.01
TINY = 1e-30

MESH = pl.DeviceIdType.MESH
F32 = jnp.float32
RELAY = 32
AHEAD = 32
STEP = 16
EARLY = 96
BF16 = jnp.bfloat16


def body(
    dims,
    p_up, g_up, m_up, r_up, c_up, p_at, g_at, m_at, r_at, c_at,
    np_up, nm_up, nr_up, nc_up, cp_up, np_at, nm_at, nr_at, nc_at, cp_at, logs,
    vg_up, vg_at, vm_up, vm_at, vp_up, vp_at, vr, vc,
    part_a, far_a, far_g, col_box,
    lane_part, rs, cs_y, cs_z, tt_y, tt_z, sq, in_sem,
    rs_send, rs_recv, cy_send, cy_recv, cz_send, cz_recv,
    ty_send, ty_recv, tz_send, tz_recv, sq_send, sq_recv,
    own_send, near_recv, far_send, far_recv, sib_send, sib_recv,
    wave_send, wave_recv, ahead_send, ahead_recv, relay_recv, box_send, box_recv, row_ready, ring_ready,
):
    ny, nz, nx = dims
    n_col = 2 * nx
    rows, cu = g_up.shape
    ca = g_at.shape[1]
    cw = cu + ca
    n_rows = rows * ny * nz
    full_up = cu * n_col
    full_at = ca * n_col

    row = lax.axis_index("row")
    col = lax.axis_index("col")
    y, z = row // nz, row % nz
    x, core = col // 2, col % 2

    col_peers = [lax.rem(col + k, n_col) for k in range(1, n_col)]
    y_peers = [lax.rem(y + k, ny) for k in range(1, ny)]
    z_peers = [lax.rem(z + k, nz) for k in sorted(range(1, nz), key=lambda k: -min(k, nz - k))]

    barrier = pltpu.get_barrier_semaphore()
    sib = (row, x * 2 + 1 - core)
    for k in range(1, nx):
        there = (row, lax.rem(x + k, nx) * 2)
        pl.semaphore_signal(barrier, inc=1, device_id=there, device_id_type=MESH)
    pl.when(core == 1)(
        lambda: pl.semaphore_signal(barrier, inc=1, device_id=sib, device_id_type=MESH)
    )
    for q in [y * nz + q for q in z_peers] + [q * nz + z for q in y_peers]:
        pl.semaphore_signal(barrier, inc=1, device_id=(q, x * 2 + 1), device_id_type=MESH)

    loads = [
        pltpu.make_async_copy(src, dst, in_sem.at[i])
        for i, (src, dst) in enumerate(
            [
                (g_up, vg_up),
                (g_at, vg_at),
                (r_up, vr.at[:, pl.ds(0, rows)]),
                (r_at, vr.at[:, pl.ds(rows, rows)]),
                (c_up, vc.at[:, pl.ds(0, cu)]),
                (c_at, vc.at[:, pl.ds(cu, ca)]),
                (m_up, vm_up),
                (p_up, vp_up),
                (m_at, vm_at),
                (p_at, vp_at),
            ]
        )
    ]
    for copy in loads:
        copy.start()

    loads[0].wait()
    loads[1].wait()
    step = 16
    acc = jnp.zeros((8, cw), F32)
    for r0 in range(0, rows, step):
        wide_u = vg_up[r0 : r0 + step, :].astype(F32)
        wide_a = vg_at[r0 : r0 + step, :].astype(F32)
        su = wide_u * wide_u + TINY
        sa = wide_a * wide_a + TINY
        both = jnp.concatenate([su, sa], axis=1)
        for s in range(0, step, 8):
            acc = acc + both[s : s + 8, :]
        lane_part[r0 : r0 + step, :] = functools.reduce(
            jnp.add, [su[:, k : k + 128] for k in range(0, cu, 128)]
        )
        lane_part[rows + r0 : rows + r0 + step, :] = functools.reduce(
            jnp.add, [sa[:, k : k + 128] for k in range(0, ca, 128)]
        )
    cs_y[y] = jnp.sum(acc, axis=0, keepdims=True)

    eye = lax.broadcasted_iota(jnp.int32, (rows, rows), 0) == lax.broadcasted_iota(
        jnp.int32, (rows, rows), 1
    )

    def to_lanes(column):
        return jnp.sum(jnp.where(eye, column, 0.0), axis=0, keepdims=True)

    def to_column(lanes):
        return jnp.sum(jnp.where(eye, lanes, 0.0), axis=1, keepdims=True)

    sums = jnp.sum(lane_part[...], axis=1, keepdims=True)
    rs[col] = jnp.concatenate([to_lanes(sums[:rows]), to_lanes(sums[rows:])], axis=1)

    @pl.when(core == 0)
    def _():
        pl.semaphore_wait(barrier, n_col - 1)
        pl.semaphore_signal(row_ready, inc=1, device_id=sib, device_id_type=MESH)

    @pl.when(core == 1)
    def _():
        pl.semaphore_wait(row_ready, 1)

    def spread(buf, slot, targets, peers, send, recv):
        out = []
        for k, (dev, peer) in enumerate(zip(targets, peers)):
            copy = pltpu.make_async_remote_copy(
                src_ref=buf.at[slot],
                dst_ref=buf.at[slot],
                send_sem=send.at[k],
                recv_sem=recv.at[slot],
                device_id=dev,
                device_id_type=MESH,
            )
            copy.start()
            out.append(copy)
        return out

    def arrive(buf, peers, recv, send):
        for peer in peers:
            pltpu.make_async_remote_copy(
                src_ref=buf.at[peer],
                dst_ref=buf.at[peer],
                send_sem=send.at[0],
                recv_sem=recv.at[peer],
                device_id=(row, col_peers[0]),
                device_id_type=MESH,
            ).wait_recv()

    def total(buf, n):
        return functools.reduce(jnp.add, [buf[k] for k in range(n)])

    col_devs = [(row, c) for c in col_peers]
    y_devs = [(q * nz + z, col) for q in y_peers]
    z_devs = [(y * nz + q, col) for q in z_peers]
    sent = []
    sent += spread(rs, col, col_devs, col_peers, rs_send, rs_recv)
    for k in range(6, 8):
        loads[k].wait()
    for r0 in range(0, EARLY, 16):
        here = slice(r0, r0 + 16)
        part_a[here, :] = (vp_up[here, :] - (RATE * BETA) * vm_up[here, :].astype(F32)).astype(BF16)


    right = (row, lax.rem(x + 1, nx) * 2 + core)
    left = (row, lax.rem(x + nx - 1, nx) * 2 + core)
    across = lax.rem(x + 2, nx) * 2 + core
    sibling = (row, x * 2 + 1 - core)
    ways = (right, left)
    half = cu // 2

    def early_copy(way, which):
        src, dst = ((part_a, far_a), (vg_up.at[pl.ds(0, EARLY), :], far_g))[which]
        return pltpu.make_async_remote_copy(
            src_ref=src,
            dst_ref=dst.at[way],
            send_sem=wave_send.at[way, which],
            recv_sem=wave_recv.at[way, which],
            device_id=ways[way],
            device_id_type=MESH,
        )


    for which in (0,):
        for way in range(2):
            copy = early_copy(way, which)
            copy.start()
            sent.append(copy)
    @pl.when(core == 1)
    def _():
        pl.semaphore_wait(barrier, 2 * ((ny - 1) + (nz - 1)))
        pl.semaphore_signal(ring_ready, inc=1, device_id=sib, device_id_type=MESH)

    @pl.when(core == 0)
    def _():
        pl.semaphore_wait(ring_ready, 1)

    sent += spread(cs_y, y, y_devs, y_peers, cy_send, cy_recv)

    for k in range(2, 6):
        loads[k].wait()
    arrive(rs, col_peers, rs_recv, rs_send)
    for which in (1,):
        for way in range(2):
            copy = early_copy(way, which)
            copy.start()
            sent.append(copy)
    full_rows = total(rs, n_col)
    old = vr[...]
    lane = lax.broadcasted_iota(jnp.int32, (1, 2 * rows), 1)
    width = jnp.where(lane < rows, 1.0 / full_up, 1.0 / full_at)
    new_rows = DECAY * old + (1.0 - DECAY) * (full_rows * width)
    nr_up[...] = new_rows[:, :rows]
    nr_at[...] = new_rows[:, rows:]
    nr_col_up = to_column(new_rows[:, :rows])
    nr_col_at = to_column(new_rows[:, rows:])
    inv_up = 1.0 / nr_col_up
    inv_at = 1.0 / nr_col_at

    acc = jnp.zeros((8, cw), F32)
    for r0 in range(0, rows, step):
        wide_u = vg_up[r0 : r0 + step, :].astype(F32)
        wide_a = vg_at[r0 : r0 + step, :].astype(F32)
        su = wide_u * wide_u * inv_up[r0 : r0 + step, :]
        sa = wide_a * wide_a * inv_at[r0 : r0 + step, :]
        both = jnp.concatenate([su, sa], axis=1)
        for s in range(0, step, 8):
            acc = acc + both[s : s + 8, :]
    tt_y[y] = jnp.concatenate([jnp.sum(acc, axis=0, keepdims=True), new_rows], axis=1)
    sent += spread(tt_y, y, y_devs, y_peers, ty_send, ty_recv)

    arrive(cs_y, y_peers, cy_recv, cy_send)
    cs_z[z] = total(cs_y, ny)
    sent += spread(cs_z, z, z_devs, z_peers, cz_send, cz_recv)

    arrive(tt_y, y_peers, ty_recv, ty_send)
    tt_z[z] = total(tt_y, ny)
    sent += spread(tt_z, z, z_devs, z_peers, tz_send, tz_recv)


    arrive(cs_z, z_peers, cz_recv, cz_send)
    new_cols = DECAY * vc[...] + (1.0 - DECAY) * (total(cs_z, nz) * (1.0 / n_rows))
    nc_up[...] = new_cols[:, :cu]
    nc_at[...] = new_cols[:, cu:]
    inv_cols = 1.0 / new_cols
    root_cols = lax.rsqrt(new_cols)
    root_up = lax.rsqrt(nr_col_up)
    root_at = lax.rsqrt(nr_col_at)
    x_devs = [(row, lax.rem(x + k, nx) * 2 + core) for k in range(1, nx)]
    if True:
        col_box[0] = root_cols[:, :cu]
        for k in range(1, nx):
            copy = pltpu.make_async_remote_copy(
                src_ref=col_box.at[0], dst_ref=col_box.at[nx - k],
                send_sem=box_send.at[k], recv_sem=box_recv.at[nx - k],
                device_id=x_devs[k - 1], device_id_type=MESH,
            )
            copy.start()
            sent.append(copy)

    arrive(tt_z, z_peers, tz_recv, tz_send)
    tt = total(tt_z, nz)
    terms = tt[:, :cw] * inv_cols
    fold = lambda v: functools.reduce(
        jnp.add, [v[:, k : k + 128] for k in range(0, v.shape[1], 128)]
    )
    sq[col] = jnp.concatenate([fold(terms[:, :cu]), fold(terms[:, cu:])], axis=1)
    sent += spread(sq, col, col_devs, col_peers, sq_send, sq_recv)
    mean_up = jnp.sum(tt[:, cw : cw + rows], axis=1, keepdims=True) * (1.0 / n_rows)
    mean_at = jnp.sum(tt[:, cw + rows :], axis=1, keepdims=True) * (1.0 / n_rows)
    for k in range(8, 10):
        loads[k].wait()
    def ahead_copy(way, which):
        box = (far_a, far_g)[which]
        rows_, cols_ = pl.ds(0, AHEAD), pl.ds(way * half, half)
        return pltpu.make_async_remote_copy(
            src_ref=box.at[way, rows_, cols_],
            dst_ref=box.at[2, rows_, cols_],
            send_sem=ahead_send.at[way, which],
            recv_sem=ahead_recv.at[way, which],
            device_id=ways[way],
            device_id_type=MESH,
        )

    for which in range(2):
        for way in range(2):
            early_copy(way, which).wait_recv()
            copy = ahead_copy(way, which)
            copy.start()
            sent.append(copy)

    arrive(sq, col_peers, sq_recv, sq_send)
    sums = total(sq, n_col)
    square_up = mean_up * (jnp.sum(sums[:, :128], axis=1, keepdims=True) * (1.0 / (n_rows * full_up)))
    square_at = mean_at * (jnp.sum(sums[:, 128:], axis=1, keepdims=True) * (1.0 / (n_rows * full_at)))
    clip_up = 1.0 / jnp.maximum(1.0, jnp.sqrt(square_up))
    clip_at = 1.0 / jnp.maximum(1.0, jnp.sqrt(square_at))
    cols_up = root_cols[:, :cu] * ((1.0 - BETA) * clip_up * jnp.sqrt(mean_up))
    cols_at = root_cols[:, cu:] * ((1.0 - BETA) * clip_at * jnp.sqrt(mean_at))

    off_up = pl.multiple_of(col * cu, cu)
    off_at = pl.multiple_of(col * ca, ca)

    def advance(up, r0, n, early=False):
        vg, vm, vp, new_p, new_m, copy_ref, root, cols, off, width = (
            (vg_up, vm_up, vp_up, np_up, nm_up, cp_up, root_up, cols_up, off_up, cu)
            if up
            else (vg_at, vm_at, vp_at, np_at, nm_at, cp_at, root_at, cols_at, off_at, ca)
        )
        for s in range(r0, r0 + n, 16):
            here = slice(s, s + 16)
            wide = vg[here, :].astype(F32)
            mom = (BETA * vm[here, :].astype(F32) + wide * root[here, :] * cols).astype(BF16)
            new_m[here, :] = mom
            param = vp[here, :] - RATE * mom.astype(F32)
            new_p[here, :] = param
            if not early:
                copy_ref[here, pl.ds(off, width)] = param.astype(BF16)

    scale_up = RATE * (1.0 - BETA) * clip_up * jnp.sqrt(mean_up)

    def finish(a_ref, g_ref, roots, owner, start, stop):
        scaled = roots * scale_up
        for r0 in range(start, stop, 16):
            here = slice(r0, r0 + 16)
            move = g_ref[here, :].astype(F32) * root_up[here, :] * scaled
            cp_up[here, pl.ds(pl.multiple_of(owner * cu, cu), cu)] = (
                a_ref[here, :].astype(F32) - move
            ).astype(BF16)

    quarter = rows // 4
    units = [[], []]
    chunks = []
    for r0 in range(EARLY, rows, STEP):
        chunks.append([(True, r0, STEP)])
        for way in range(2):
            units[way].append((True, r0, STEP, way * half, half))
    for k in range(2):
        chunks.append([(False, (2 * way + k) * quarter, quarter) for way in range(2)])
        for way in range(2):
            units[way].append((False, (2 * way + k) * quarter, quarter, 0, ca))
    n_late = len(chunks)

    def view(unit, owner):
        up, r0, n, c0, w = unit
        ref, width = (cp_up, cu) if up else (cp_at, ca)
        return ref.at[pl.ds(r0, n), pl.ds(pl.multiple_of(owner * width + c0, w), w)]

    def block(up, owner):
        if up:
            return cp_up.at[:, pl.ds(pl.multiple_of(owner * cu, cu), cu)]
        return cp_at.at[:, pl.ds(pl.multiple_of(owner * ca, ca), ca)]

    def push(piece, owner, dev, send, recv):
        pltpu.make_async_remote_copy(
            src_ref=view(piece, owner),
            dst_ref=view(piece, owner),
            send_sem=send,
            recv_sem=recv,
            device_id=dev,
            device_id_type=MESH,
        ).start()

    def await_recv(ref, recv):
        pltpu.make_async_remote_copy(
            src_ref=ref, dst_ref=ref, send_sem=sib_send.at[0, 0], recv_sem=recv,
            device_id=sibling, device_id_type=MESH,
        ).wait_recv()

    def await_send(ref, send):
        pltpu.make_async_remote_copy(
            src_ref=ref, dst_ref=ref, send_sem=send, recv_sem=far_recv.at[0, 0],
            device_id=sibling, device_id_type=MESH,
        ).wait_send()

    kind = lambda unit: 0 if unit[0] else 1

    def to_sibling(unit, owner, k):
        push(unit, owner, sibling, sib_send.at[k, kind(unit)], sib_recv.at[k, kind(unit)])

    def near(way, part, i):
        unit = units[part][i]
        push(unit, col, ways[way], own_send.at[way, kind(unit)], near_recv.at[way, part, i])

    for i in range(n_late):
        for up, r0, n in chunks[i]:
            advance(up, r0, n)
        near(0, 0, i)
        near(1, 1, i)
    for i in range(n_late):
        near(0, 1, i)
        near(1, 0, i)
        for up, r0, n in chunks[i]:
            to_sibling((up, r0, n, 0, cu if up else ca), col, 0)

    lane4 = lax.broadcasted_iota(jnp.int32, (1, 128), 1)
    four = jnp.where(
        lane4 == 0, mean_up, jnp.where(lane4 == 1, mean_at, jnp.where(lane4 == 2, square_up, square_at))
    )
    logs[...] = jnp.log(four)[:, :4]

    left_col, right_col = left[1], right[1]
    if EARLY:
        for k in range(1, nx):
            pltpu.make_async_remote_copy(
                src_ref=col_box.at[0], dst_ref=col_box.at[k],
                send_sem=box_send.at[k], recv_sem=box_recv.at[k],
                device_id=x_devs[0], device_id_type=MESH,
            ).wait_recv()

    from_cols = (left_col, right_col)
    roots_of = (col_box[nx - 1], col_box[1])
    marks = list(range(AHEAD, EARLY, RELAY))
    for c, r0 in enumerate(marks):
        for way in range(2):
            finish(far_a.at[way], far_g.at[way], roots_of[way], from_cols[way], r0, r0 + RELAY)
            push((True, r0, RELAY, way * half, half), from_cols[way], ways[way], far_send.at[way, 0], relay_recv.at[way, c])
    for way in range(2):
        finish(far_a.at[way], far_g.at[way], roots_of[way], from_cols[way], 0, AHEAD)
        to_sibling((True, 0, EARLY, 0, cu), from_cols[way], way + 1)
    advance(True, 0, EARLY, early=True)
    finish(part_a, vg_up, col_box[0], col, 0, EARLY)
    to_sibling((True, 0, EARLY, 0, cu), col, 0)
    for i in range(n_late):
        for way in range(2):
            unit, owner = units[way][i], from_cols[way]
            await_recv(view(unit, owner), near_recv.at[way, way, i])
            push(unit, owner, ways[way], far_send.at[way, kind(unit)], far_recv.at[way, i])
            to_sibling(unit, owner, way + 1)
    for copy in sent:
        copy.wait_send()
    for which in range(2):
        for way in range(2):
            ahead_copy(way, which).wait_recv()
    finish(far_a.at[2], far_g.at[2], col_box[2], across, 0, AHEAD)
    to_sibling((True, 0, AHEAD, 0, cu), across, 3)
    for c, r0 in enumerate(marks):
        for way in range(2):
            unit = (True, r0, RELAY, way * half, half)
            await_recv(view(unit, across), relay_recv.at[way, c])
            to_sibling(unit, across, 3)
    for i in range(n_late):
        for way in range(2):
            unit = units[way][i]
            await_recv(view(unit, across), far_recv.at[way, i])
            to_sibling(unit, across, 3)
        for way in range(2):
            unit = units[1 - way][i]
            await_recv(view(unit, from_cols[way]), near_recv.at[way, 1 - way, i])
            to_sibling(unit, from_cols[way], way + 1)

    late = rows - EARLY
    for side in range(2):
        for t, (ref, n, w) in enumerate(((cp_up, late, cu), (cp_at, rows, ca))):
            here = pl.ds(pl.multiple_of(col * w, w), w)
            await_send(ref.at[pl.ds(0, n), here], own_send.at[side, t])
            here = pl.ds(pl.multiple_of(col * w, w // 2), w // 2)
            await_send(ref.at[pl.ds(0, (rows - AHEAD, rows)[t]), here], far_send.at[side, t])
    other = lambda c: c + 1 - 2 * core
    owners = [col, left_col, right_col, across]
    for k, owner in enumerate(owners):
        for t, up in enumerate((True, False)):
            await_send(block(up, owner), sib_send.at[k, t])
            await_recv(block(up, other(owner)), sib_recv.at[k, t])


def write_out(*refs):
    n = (len(refs) - 1) // 2
    sems = refs[-1]
    copies = [
        pltpu.make_async_copy(src, dst, sems.at[i])
        for i, (src, dst) in enumerate(zip(refs[:n], refs[n : 2 * n]))
    ]
    for copy in copies:
        copy.start()
    for copy in copies:
        copy.wait()


def on_device(
    dims, p_up, g_up, m_up, r_up, c_up, p_at, g_at, m_at, r_at, c_at
):
    ny, nz, nx = dims
    n_col = 2 * nx
    rows, cu = g_up.shape
    ca = g_at.shape[1]
    cw = cu + ca
    n_late = (rows - EARLY) // STEP + 2
    dma = pltpu.SemaphoreType.DMA
    vm = pltpu.VMEM
    scratch = [
        vm((rows, cu), BF16), vm((rows, ca), BF16),
        vm((rows, cu), BF16), vm((rows, ca), BF16),
        vm((rows, cu), F32), vm((rows, ca), F32),
        vm((1, 2 * rows), F32), vm((1, cw), F32),
        vm((EARLY, cu), BF16), vm((3, EARLY, cu), BF16), vm((3, EARLY, cu), BF16), vm((nx, 1, cu), F32),
        vm((2 * rows, 128), F32),
        vm((n_col, 1, 2 * rows), F32),
        vm((ny, 1, cw), F32), vm((nz, 1, cw), F32),
        vm((ny, 1, cw + 2 * rows), F32), vm((nz, 1, cw + 2 * rows), F32),
        vm((n_col, 1, 256), F32),
        dma((10,)),
        dma((n_col - 1,)), dma((n_col,)),
        dma((max(ny - 1, 1),)), dma((ny,)),
        dma((max(nz - 1, 1),)), dma((nz,)),
        dma((max(ny - 1, 1),)), dma((ny,)),
        dma((max(nz - 1, 1),)), dma((nz,)),
        dma((n_col - 1,)), dma((n_col,)),
        dma((2, 2)), dma((2, 2, n_late)), dma((2, 2)), dma((2, n_late)), dma((4, 2)), dma((4, 2)),
        dma((2, 2)), dma((2, 2)), dma((2, 2)), dma((2, 2)), dma((2, (EARLY - AHEAD) // RELAY)),
        dma((nx,)), dma((nx,)),
        pltpu.SemaphoreType.REGULAR, pltpu.SemaphoreType.REGULAR,
    ]
    out_shape = [
        vm((rows, cu), F32), vm((rows, cu), BF16), vm((1, rows), F32), vm((1, cu), F32),
        vm((rows, cu * n_col), BF16),
        vm((rows, ca), F32), vm((rows, ca), BF16), vm((1, rows), F32), vm((1, ca), F32),
        vm((rows, ca * n_col), BF16),
        vm((1, 4), F32),
    ]
    anywhere = pl.BlockSpec(memory_space=pltpu.HBM)
    inside = pl.BlockSpec(memory_space=pltpu.VMEM)
    results = pl.pallas_call(
        functools.partial(body, dims),
        out_shape=out_shape,
        in_specs=[anywhere] * 10,
        out_specs=[inside] * 11,
        scratch_shapes=scratch,
        compiler_params=pltpu.CompilerParams(
            collective_id=0, has_side_effects=True, vmem_limit_bytes=40 * 1024 * 1024
        ),
        cost_estimate=pl.CostEstimate(
            flops=20 * rows * cw, bytes_accessed=10 * rows * cw, transcendentals=0
        ),
    )(
        *[
            pltpu.with_memory_space_constraint(a, pltpu.HBM)
            for a in (
                p_up, g_up, m_up, r_up.reshape(1, rows), c_up.reshape(1, cu),
                p_at, g_at, m_at, r_at.reshape(1, rows), c_at.reshape(1, ca),
            )
        ]
    )
    (np_up, nm_up, nr_up, nc_up, cp_up, np_at, nm_at, nr_at, nc_at, cp_at, logs) = pl.pallas_call(
        write_out,
        out_shape=[pltpu.HBM(o.shape, o.dtype) for o in out_shape],
        in_specs=[inside] * 11,
        out_specs=[anywhere] * 11,
        scratch_shapes=[dma((11,))],
        compiler_params=pltpu.CompilerParams(vmem_limit_bytes=1024 * 1024),
        cost_estimate=pl.CostEstimate(
            flops=0, bytes_accessed=2 * rows * cw * (n_col + 3), transcendentals=0
        ),
    )(*[pltpu.with_memory_space_constraint(r, pltpu.VMEM) for r in results])
    return (
        np_up, nm_up, nr_up.reshape(rows), nc_up.reshape(cu), cp_up,
        np_at, nm_at, nr_at.reshape(rows), nc_at.reshape(ca), cp_at,
        logs.reshape(4),
    )


def solution(mesh, dims=(4, 8, 4)):
    block = P("row", "col")
    in_specs = (block, block, block, P("row"), P("col")) * 2
    out_specs = (block, block, P("row"), P("col"), P("row", None)) * 2 + (P(),)
    return jax.shard_map(
        functools.partial(on_device, dims),
        mesh=mesh,
        in_specs=in_specs,
        out_specs=out_specs,
        check_vma=False,
    )
```

```python
import functools

import jax
import jax.numpy as jnp
from jax import lax
from jax.experimental import pallas as pl
from jax.experimental.pallas import tpu as pltpu
from jax.sharding import PartitionSpec as P

DECAY = 0.8415
BETA = 0.9
RATE = 0.01
TINY = 1e-30

MESH = pl.DeviceIdType.MESH
F32 = jnp.float32
RELAY = 32
AHEAD = 32
STEP = 16
EARLY = 96
BF16 = jnp.bfloat16


def body(
    dims,
    p_up, g_up, m_up, r_up, c_up, p_at, g_at, m_at, r_at, c_at,
    np_up, nm_up, nr_up, nc_up, cp_up, np_at, nm_at, nr_at, nc_at, cp_at, logs,
    vg_up, vg_at, vm_up, vm_at, vp_up, vp_at, vr, vc,
    part_a, far_a, far_g, col_box,
    lane_part, rs, cs_y, cs_z, tt_y, tt_z, sq, in_sem,
    rs_send, rs_recv, cy_send, cy_recv, cz_send, cz_recv,
    ty_send, ty_recv, tz_send, tz_recv, sq_send, sq_recv,
    own_send, near_recv, far_send, far_recv, sib_send, sib_recv,
    wave_send, wave_recv, ahead_send, ahead_recv, relay_recv, box_send, box_recv, row_ready, ring_ready,
):
    ny, nz, nx = dims
    n_col = 2 * nx
    rows, cu = g_up.shape
    ca = g_at.shape[1]
    cw = cu + ca
    n_rows = rows * ny * nz
    full_up = cu * n_col
    full_at = ca * n_col

    row = lax.axis_index("row")
    col = lax.axis_index("col")
    y, z = row // nz, row % nz
    x, core = col // 2, col % 2

    col_peers = [lax.rem(col + k, n_col) for k in range(1, n_col)]
    y_peers = [lax.rem(y + k, ny) for k in range(1, ny)]
    z_peers = [lax.rem(z + k, nz) for k in sorted(range(1, nz), key=lambda k: -min(k, nz - k))]

    barrier = pltpu.get_barrier_semaphore()
    sib = (row, x * 2 + 1 - core)
    for k in range(1, nx):
        there = (row, lax.rem(x + k, nx) * 2)
        pl.semaphore_signal(barrier, inc=1, device_id=there, device_id_type=MESH)
    pl.when(core == 1)(
        lambda: pl.semaphore_signal(barrier, inc=1, device_id=sib, device_id_type=MESH)
    )
    for q in [y * nz + q for q in z_peers] + [q * nz + z for q in y_peers]:
        pl.semaphore_signal(barrier, inc=1, device_id=(q, x * 2 + 1), device_id_type=MESH)

    loads = [
        pltpu.make_async_copy(src, dst, in_sem.at[i])
        for i, (src, dst) in enumerate(
            [
                (g_up, vg_up),
                (g_at, vg_at),
                (r_up, vr.at[:, pl.ds(0, rows)]),
                (r_at, vr.at[:, pl.ds(rows, rows)]),
                (c_up, vc.at[:, pl.ds(0, cu)]),
                (c_at, vc.at[:, pl.ds(cu, ca)]),
                (m_up, vm_up),
                (p_up, vp_up),
                (m_at, vm_at),
                (p_at, vp_at),
            ]
        )
    ]
    for copy in loads:
        copy.start()

    loads[0].wait()
    loads[1].wait()
    step = 16
    acc = jnp.zeros((8, cw), F32)
    for r0 in range(0, rows, step):
        wide_u = vg_up[r0 : r0 + step, :].astype(F32)
        wide_a = vg_at[r0 : r0 + step, :].astype(F32)
        su = wide_u * wide_u + TINY
        sa = wide_a * wide_a + TINY
        both = jnp.concatenate([su, sa], axis=1)
        for s in range(0, step, 8):
            acc = acc + both[s : s + 8, :]
        lane_part[r0 : r0 + step, :] = functools.reduce(
            jnp.add, [su[:, k : k + 128] for k in range(0, cu, 128)]
        )
        lane_part[rows + r0 : rows + r0 + step, :] = functools.reduce(
            jnp.add, [sa[:, k : k + 128] for k in range(0, ca, 128)]
        )
    cs_y[y] = jnp.sum(acc, axis=0, keepdims=True)

    eye = lax.broadcasted_iota(jnp.int32, (rows, rows), 0) == lax.broadcasted_iota(
        jnp.int32, (rows, rows), 1
    )

    def to_lanes(column):
        return jnp.sum(jnp.where(eye, column, 0.0), axis=0, keepdims=True)

    def to_column(lanes):
        return jnp.sum(jnp.where(eye, lanes, 0.0), axis=1, keepdims=True)

    sums = jnp.sum(lane_part[...], axis=1, keepdims=True)
    rs[col] = jnp.concatenate([to_lanes(sums[:rows]), to_lanes(sums[rows:])], axis=1)

    @pl.when(core == 0)
    def _():
        pl.semaphore_wait(barrier, n_col - 1)
        pl.semaphore_signal(row_ready, inc=1, device_id=sib, device_id_type=MESH)

    @pl.when(core == 1)
    def _():
        pl.semaphore_wait(row_ready, 1)

    def spread(buf, slot, targets, peers, send, recv):
        out = []
        for k, (dev, peer) in enumerate(zip(targets, peers)):
            copy = pltpu.make_async_remote_copy(
                src_ref=buf.at[slot],
                dst_ref=buf.at[slot],
                send_sem=send.at[k],
                recv_sem=recv.at[slot],
                device_id=dev,
                device_id_type=MESH,
            )
            copy.start()
            out.append(copy)
        return out

    def arrive(buf, peers, recv, send):
        for peer in peers:
            pltpu.make_async_remote_copy(
                src_ref=buf.at[peer],
                dst_ref=buf.at[peer],
                send_sem=send.at[0],
                recv_sem=recv.at[peer],
                device_id=(row, col_peers[0]),
                device_id_type=MESH,
            ).wait_recv()

    def total(buf, n):
        return functools.reduce(jnp.add, [buf[k] for k in range(n)])

    col_devs = [(row, c) for c in col_peers]
    y_devs = [(q * nz + z, col) for q in y_peers]
    z_devs = [(y * nz + q, col) for q in z_peers]
    sent = []
    sent += spread(rs, col, col_devs, col_peers, rs_send, rs_recv)
    for k in range(6, 8):
        loads[k].wait()
    for r0 in range(0, EARLY, 16):
        here = slice(r0, r0 + 16)
        part_a[here, :] = (vp_up[here, :] - (RATE * BETA) * vm_up[here, :].astype(F32)).astype(BF16)


    right = (row, lax.rem(x + 1, nx) * 2 + core)
    left = (row, lax.rem(x + nx - 1, nx) * 2 + core)
    across = lax.rem(x + 2, nx) * 2 + core
    sibling = (row, x * 2 + 1 - core)
    ways = (right, left)
    half = cu // 2

    def early_copy(way, which):
        src, dst = ((part_a, far_a), (vg_up.at[pl.ds(0, EARLY), :], far_g))[which]
        return pltpu.make_async_remote_copy(
            src_ref=src,
            dst_ref=dst.at[way],
            send_sem=wave_send.at[way, which],
            recv_sem=wave_recv.at[way, which],
            device_id=ways[way],
            device_id_type=MESH,
        )


    for which in (0,):
        for way in range(2):
            copy = early_copy(way, which)
            copy.start()
            sent.append(copy)
    @pl.when(core == 1)
    def _():
        pl.semaphore_wait(barrier, 2 * ((ny - 1) + (nz - 1)))
        pl.semaphore_signal(ring_ready, inc=1, device_id=sib, device_id_type=MESH)

    @pl.when(core == 0)
    def _():
        pl.semaphore_wait(ring_ready, 1)

    sent += spread(cs_y, y, y_devs, y_peers, cy_send, cy_recv)

    for k in range(2, 6):
        loads[k].wait()
    arrive(rs, col_peers, rs_recv, rs_send)
    for which in (1,):
        for way in range(2):
            copy = early_copy(way, which)
            copy.start()
            sent.append(copy)
    full_rows = total(rs, n_col)
    old = vr[...]
    lane = lax.broadcasted_iota(jnp.int32, (1, 2 * rows), 1)
    width = jnp.where(lane < rows, 1.0 / full_up, 1.0 / full_at)
    new_rows = DECAY * old + (1.0 - DECAY) * (full_rows * width)
    nr_up[...] = new_rows[:, :rows]
    nr_at[...] = new_rows[:, rows:]
    nr_col_up = to_column(new_rows[:, :rows])
    nr_col_at = to_column(new_rows[:, rows:])
    inv_up = 1.0 / nr_col_up
    inv_at = 1.0 / nr_col_at

    acc = jnp.zeros((8, cw), F32)
    for r0 in range(0, rows, step):
        wide_u = vg_up[r0 : r0 + step, :].astype(F32)
        wide_a = vg_at[r0 : r0 + step, :].astype(F32)
        su = wide_u * wide_u * inv_up[r0 : r0 + step, :]
        sa = wide_a * wide_a * inv_at[r0 : r0 + step, :]
        both = jnp.concatenate([su, sa], axis=1)
        for s in range(0, step, 8):
            acc = acc + both[s : s + 8, :]
    tt_y[y] = jnp.concatenate([jnp.sum(acc, axis=0, keepdims=True), new_rows], axis=1)
    sent += spread(tt_y, y, y_devs, y_peers, ty_send, ty_recv)

    arrive(cs_y, y_peers, cy_recv, cy_send)
    cs_z[z] = total(cs_y, ny)
    sent += spread(cs_z, z, z_devs, z_peers, cz_send, cz_recv)

    arrive(tt_y, y_peers, ty_recv, ty_send)
    tt_z[z] = total(tt_y, ny)
    sent += spread(tt_z, z, z_devs, z_peers, tz_send, tz_recv)


    arrive(cs_z, z_peers, cz_recv, cz_send)
    new_cols = DECAY * vc[...] + (1.0 - DECAY) * (total(cs_z, nz) * (1.0 / n_rows))
    nc_up[...] = new_cols[:, :cu]
    nc_at[...] = new_cols[:, cu:]
    inv_cols = 1.0 / new_cols
    root_cols = lax.rsqrt(new_cols)
    root_up = lax.rsqrt(nr_col_up)
    root_at = lax.rsqrt(nr_col_at)
    x_devs = [(row, lax.rem(x + k, nx) * 2 + core) for k in range(1, nx)]
    if True:
        col_box[0] = root_cols[:, :cu]
        for k in range(1, nx):
            copy = pltpu.make_async_remote_copy(
                src_ref=col_box.at[0], dst_ref=col_box.at[nx - k],
                send_sem=box_send.at[k], recv_sem=box_recv.at[nx - k],
                device_id=x_devs[k - 1], device_id_type=MESH,
            )
            copy.start()
            sent.append(copy)

    arrive(tt_z, z_peers, tz_recv, tz_send)
    tt = total(tt_z, nz)
    terms = tt[:, :cw] * inv_cols
    fold = lambda v: functools.reduce(
        jnp.add, [v[:, k : k + 128] for k in range(0, v.shape[1], 128)]
    )
    sq[col] = jnp.concatenate([fold(terms[:, :cu]), fold(terms[:, cu:])], axis=1)
    sent += spread(sq, col, col_devs, col_peers, sq_send, sq_recv)
    mean_up = jnp.sum(tt[:, cw : cw + rows], axis=1, keepdims=True) * (1.0 / n_rows)
    mean_at = jnp.sum(tt[:, cw + rows :], axis=1, keepdims=True) * (1.0 / n_rows)
    for k in range(8, 10):
        loads[k].wait()
    def ahead_copy(way, which):
        box = (far_a, far_g)[which]
        rows_, cols_ = pl.ds(0, AHEAD), pl.ds(way * half, half)
        return pltpu.make_async_remote_copy(
            src_ref=box.at[way, rows_, cols_],
            dst_ref=box.at[2, rows_, cols_],
            send_sem=ahead_send.at[way, which],
            recv_sem=ahead_recv.at[way, which],
            device_id=ways[way],
            device_id_type=MESH,
        )

    for which in range(2):
        for way in range(2):
            early_copy(way, which).wait_recv()
            copy = ahead_copy(way, which)
            copy.start()
            sent.append(copy)

    arrive(sq, col_peers, sq_recv, sq_send)
    sums = total(sq, n_col)
    square_up = mean_up * (jnp.sum(sums[:, :128], axis=1, keepdims=True) * (1.0 / (n_rows * full_up)))
    square_at = mean_at * (jnp.sum(sums[:, 128:], axis=1, keepdims=True) * (1.0 / (n_rows * full_at)))
    clip_up = 1.0 / jnp.maximum(1.0, jnp.sqrt(square_up))
    clip_at = 1.0 / jnp.maximum(1.0, jnp.sqrt(square_at))
    cols_up = root_cols[:, :cu] * ((1.0 - BETA) * clip_up * jnp.sqrt(mean_up))
    cols_at = root_cols[:, cu:] * ((1.0 - BETA) * clip_at * jnp.sqrt(mean_at))

    off_up = pl.multiple_of(col * cu, cu)
    off_at = pl.multiple_of(col * ca, ca)

    def advance(up, r0, n, early=False):
        vg, vm, vp, new_p, new_m, copy_ref, root, cols, off, width = (
            (vg_up, vm_up, vp_up, np_up, nm_up, cp_up, root_up, cols_up, off_up, cu)
            if up
            else (vg_at, vm_at, vp_at, np_at, nm_at, cp_at, root_at, cols_at, off_at, ca)
        )
        for s in range(r0, r0 + n, 16):
            here = slice(s, s + 16)
            wide = vg[here, :].astype(F32)
            mom = (BETA * vm[here, :].astype(F32) + wide * root[here, :] * cols).astype(BF16)
            new_m[here, :] = mom
            param = vp[here, :] - RATE * mom.astype(F32)
            new_p[here, :] = param
            if not early:
                copy_ref[here, pl.ds(off, width)] = param.astype(BF16)

    scale_up = RATE * (1.0 - BETA) * clip_up * jnp.sqrt(mean_up)

    def finish(a_ref, g_ref, roots, owner, start, stop):
        scaled = roots * scale_up
        for r0 in range(start, stop, 16):
            here = slice(r0, r0 + 16)
            move = g_ref[here, :].astype(F32) * root_up[here, :] * scaled
            cp_up[here, pl.ds(pl.multiple_of(owner * cu, cu), cu)] = (
                a_ref[here, :].astype(F32) - move
            ).astype(BF16)

    quarter = rows // 4
    units = [[], []]
    chunks = []
    for r0 in range(EARLY, rows, STEP):
        chunks.append([(True, r0, STEP)])
        for way in range(2):
            units[way].append((True, r0, STEP, way * half, half))
    for k in range(2):
        chunks.append([(False, (2 * way + k) * quarter, quarter) for way in range(2)])
        for way in range(2):
            units[way].append((False, (2 * way + k) * quarter, quarter, 0, ca))
    n_late = len(chunks)

    def view(unit, owner):
        up, r0, n, c0, w = unit
        ref, width = (cp_up, cu) if up else (cp_at, ca)
        return ref.at[pl.ds(r0, n), pl.ds(pl.multiple_of(owner * width + c0, w), w)]

    def block(up, owner):
        if up:
            return cp_up.at[:, pl.ds(pl.multiple_of(owner * cu, cu), cu)]
        return cp_at.at[:, pl.ds(pl.multiple_of(owner * ca, ca), ca)]

    def push(piece, owner, dev, send, recv):
        pltpu.make_async_remote_copy(
            src_ref=view(piece, owner),
            dst_ref=view(piece, owner),
            send_sem=send,
            recv_sem=recv,
            device_id=dev,
            device_id_type=MESH,
        ).start()

    def await_recv(ref, recv):
        pltpu.make_async_remote_copy(
            src_ref=ref, dst_ref=ref, send_sem=sib_send.at[0, 0], recv_sem=recv,
            device_id=sibling, device_id_type=MESH,
        ).wait_recv()

    def await_send(ref, send):
        pltpu.make_async_remote_copy(
            src_ref=ref, dst_ref=ref, send_sem=send, recv_sem=far_recv.at[0, 0],
            device_id=sibling, device_id_type=MESH,
        ).wait_send()

    kind = lambda unit: 0 if unit[0] else 1

    def to_sibling(unit, owner, k):
        push(unit, owner, sibling, sib_send.at[k, kind(unit)], sib_recv.at[k, kind(unit)])

    def near(way, part, i):
        unit = units[part][i]
        push(unit, col, ways[way], own_send.at[way, kind(unit)], near_recv.at[way, part, i])

    for i in range(n_late):
        for up, r0, n in chunks[i]:
            advance(up, r0, n)
        near(0, 0, i)
        near(1, 1, i)
    for i in range(n_late):
        for up, r0, n in chunks[i]:
            to_sibling((up, r0, n, 0, cu if up else ca), col, 0)

    lane4 = lax.broadcasted_iota(jnp.int32, (1, 128), 1)
    four = jnp.where(
        lane4 == 0, mean_up, jnp.where(lane4 == 1, mean_at, jnp.where(lane4 == 2, square_up, square_at))
    )
    logs[...] = jnp.log(four)[:, :4]

    left_col, right_col = left[1], right[1]
    if EARLY:
        for k in range(1, nx):
            pltpu.make_async_remote_copy(
                src_ref=col_box.at[0], dst_ref=col_box.at[k],
                send_sem=box_send.at[k], recv_sem=box_recv.at[k],
                device_id=x_devs[0], device_id_type=MESH,
            ).wait_recv()

    from_cols = (left_col, right_col)
    roots_of = (col_box[nx - 1], col_box[1])
    marks = list(range(AHEAD, EARLY, RELAY))
    for c, r0 in enumerate(marks):
        for way in range(2):
            finish(far_a.at[way], far_g.at[way], roots_of[way], from_cols[way], r0, r0 + RELAY)
            push((True, r0, RELAY, way * half, half), from_cols[way], ways[way], far_send.at[way, 0], relay_recv.at[way, c])
    for way in range(2):
        finish(far_a.at[way], far_g.at[way], roots_of[way], from_cols[way], 0, AHEAD)
        to_sibling((True, 0, EARLY, 0, cu), from_cols[way], way + 1)
    advance(True, 0, EARLY, early=True)
    finish(part_a, vg_up, col_box[0], col, 0, EARLY)
    to_sibling((True, 0, EARLY, 0, cu), col, 0)
    for i in range(n_late):
        for way in range(2):
            unit, owner = units[way][i], from_cols[way]
            await_recv(view(unit, owner), near_recv.at[way, way, i])
            push(unit, owner, ways[way], far_send.at[way, kind(unit)], far_recv.at[way, i])
            near(way, 1 - way, i)
            to_sibling(unit, owner, way + 1)
    for copy in sent:
        copy.wait_send()
    for which in range(2):
        for way in range(2):
            ahead_copy(way, which).wait_recv()
    finish(far_a.at[2], far_g.at[2], col_box[2], across, 0, AHEAD)
    to_sibling((True, 0, AHEAD, 0, cu), across, 3)
    for c, r0 in enumerate(marks):
        for way in range(2):
            unit = (True, r0, RELAY, way * half, half)
            await_recv(view(unit, across), relay_recv.at[way, c])
            to_sibling(unit, across, 3)
    for i in range(n_late):
        for way in range(2):
            unit = units[way][i]
            await_recv(view(unit, across), far_recv.at[way, i])
            to_sibling(unit, across, 3)
        for way in range(2):
            unit = units[1 - way][i]
            await_recv(view(unit, from_cols[way]), near_recv.at[way, 1 - way, i])
            to_sibling(unit, from_cols[way], way + 1)

    late = rows - EARLY
    for side in range(2):
        for t, (ref, n, w) in enumerate(((cp_up, late, cu), (cp_at, rows, ca))):
            here = pl.ds(pl.multiple_of(col * w, w), w)
            await_send(ref.at[pl.ds(0, n), here], own_send.at[side, t])
            here = pl.ds(pl.multiple_of(col * w, w // 2), w // 2)
            await_send(ref.at[pl.ds(0, (rows - AHEAD, rows)[t]), here], far_send.at[side, t])
    other = lambda c: c + 1 - 2 * core
    owners = [col, left_col, right_col, across]
    for k, owner in enumerate(owners):
        for t, up in enumerate((True, False)):
            await_send(block(up, owner), sib_send.at[k, t])
            await_recv(block(up, other(owner)), sib_recv.at[k, t])


def write_out(*refs):
    n = (len(refs) - 1) // 2
    sems = refs[-1]
    copies = [
        pltpu.make_async_copy(src, dst, sems.at[i])
        for i, (src, dst) in enumerate(zip(refs[:n], refs[n : 2 * n]))
    ]
    copies.sort(key=lambda copy: -copy.src_ref.shape[1])
    for copy in copies:
        copy.start()
    for copy in copies:
        copy.wait()


def on_device(
    dims, p_up, g_up, m_up, r_up, c_up, p_at, g_at, m_at, r_at, c_at
):
    ny, nz, nx = dims
    n_col = 2 * nx
    rows, cu = g_up.shape
    ca = g_at.shape[1]
    cw = cu + ca
    n_late = (rows - EARLY) // STEP + 2
    dma = pltpu.SemaphoreType.DMA
    vm = pltpu.VMEM
    scratch = [
        vm((rows, cu), BF16), vm((rows, ca), BF16),
        vm((rows, cu), BF16), vm((rows, ca), BF16),
        vm((rows, cu), F32), vm((rows, ca), F32),
        vm((1, 2 * rows), F32), vm((1, cw), F32),
        vm((EARLY, cu), BF16), vm((3, EARLY, cu), BF16), vm((3, EARLY, cu), BF16), vm((nx, 1, cu), F32),
        vm((2 * rows, 128), F32),
        vm((n_col, 1, 2 * rows), F32),
        vm((ny, 1, cw), F32), vm((nz, 1, cw), F32),
        vm((ny, 1, cw + 2 * rows), F32), vm((nz, 1, cw + 2 * rows), F32),
        vm((n_col, 1, 256), F32),
        dma((10,)),
        dma((n_col - 1,)), dma((n_col,)),
        dma((max(ny - 1, 1),)), dma((ny,)),
        dma((max(nz - 1, 1),)), dma((nz,)),
        dma((max(ny - 1, 1),)), dma((ny,)),
        dma((max(nz - 1, 1),)), dma((nz,)),
        dma((n_col - 1,)), dma((n_col,)),
        dma((2, 2)), dma((2, 2, n_late)), dma((2, 2)), dma((2, n_late)), dma((4, 2)), dma((4, 2)),
        dma((2, 2)), dma((2, 2)), dma((2, 2)), dma((2, 2)), dma((2, (EARLY - AHEAD) // RELAY)),
        dma((nx,)), dma((nx,)),
        pltpu.SemaphoreType.REGULAR, pltpu.SemaphoreType.REGULAR,
    ]
    out_shape = [
        vm((rows, cu), F32), vm((rows, cu), BF16), vm((1, rows), F32), vm((1, cu), F32),
        vm((rows, cu * n_col), BF16),
        vm((rows, ca), F32), vm((rows, ca), BF16), vm((1, rows), F32), vm((1, ca), F32),
        vm((rows, ca * n_col), BF16),
        vm((1, 4), F32),
    ]
    anywhere = pl.BlockSpec(memory_space=pltpu.HBM)
    inside = pl.BlockSpec(memory_space=pltpu.VMEM)
    results = pl.pallas_call(
        functools.partial(body, dims),
        out_shape=out_shape,
        in_specs=[anywhere] * 10,
        out_specs=[inside] * 11,
        scratch_shapes=scratch,
        compiler_params=pltpu.CompilerParams(
            collective_id=0, has_side_effects=True, vmem_limit_bytes=40 * 1024 * 1024
        ),
        cost_estimate=pl.CostEstimate(
            flops=20 * rows * cw, bytes_accessed=10 * rows * cw, transcendentals=0
        ),
    )(
        *[
            pltpu.with_memory_space_constraint(a, pltpu.HBM)
            for a in (
                p_up, g_up, m_up, r_up.reshape(1, rows), c_up.reshape(1, cu),
                p_at, g_at, m_at, r_at.reshape(1, rows), c_at.reshape(1, ca),
            )
        ]
    )
    (np_up, nm_up, nr_up, nc_up, cp_up, np_at, nm_at, nr_at, nc_at, cp_at, logs) = pl.pallas_call(
        write_out,
        out_shape=[pltpu.HBM(o.shape, o.dtype) for o in out_shape],
        in_specs=[inside] * 11,
        out_specs=[anywhere] * 11,
        scratch_shapes=[dma((11,))],
        compiler_params=pltpu.CompilerParams(vmem_limit_bytes=1024 * 1024),
        cost_estimate=pl.CostEstimate(
            flops=0, bytes_accessed=2 * rows * cw * (n_col + 3), transcendentals=0
        ),
    )(*[pltpu.with_memory_space_constraint(r, pltpu.VMEM) for r in results])
    return (
        np_up, nm_up, nr_up.reshape(rows), nc_up.reshape(cu), cp_up,
        np_at, nm_at, nr_at.reshape(rows), nc_at.reshape(ca), cp_at,
        logs.reshape(4),
    )


def solution(mesh, dims=(4, 8, 4)):
    block = P("row", "col")
    in_specs = (block, block, block, P("row"), P("col")) * 2
    out_specs = (block, block, P("row"), P("col"), P("row", None)) * 2 + (P(),)
    return jax.shard_map(
        functools.partial(on_device, dims),
        mesh=mesh,
        in_specs=in_specs,
        out_specs=out_specs,
        check_vma=False,
    )
```
